32 devices in a mesh: group: 2 (over x), patch: 8 (over z, y), uly: 2 (over core).
Axes of the slice: x: 2, y: 2, z: 4, core: 2. Of those that a mesh axis runs over, the one named last changes fastest.
Arguments:
- fresh_first: bfloat16 [3, 1536, 1536], P(None, ('group', 'patch', 'uly')), parts along dimension 1, may hold values from -200 to 200
- fresh_second: bfloat16 [3, 1536, 1536], P(None, ('group', 'patch', 'uly')), parts along dimension 1, may hold values from -200 to 200
- stale_cache: bfloat16 [2, 1536, 1536], P(None, ('group', 'patch'), 'uly'), parts along dimension 1, may hold values from -40 to 40
- stale_exponent: int32 [4, 12], P('group'), parts along dimension 0, may hold values from -2 to 1
- text_first: bfloat16 [2, 512, 1536], P(None, 'group', 'uly'), parts along dimension 1, may hold values from -40 to 40
- text_second: bfloat16 [2, 512, 1536], P(None, 'group', 'uly'), parts along dimension 1, may hold values from -40 to 40
Outputs:
- attended_first: bfloat16 [1536, 1536], P(('group', 'patch', 'uly')), parts along dimension 0
- attended_second: bfloat16 [1536, 1536], P(('group', 'patch', 'uly')), parts along dimension 0
The draws below stay inside these ranges and needn't reach their ends.
There are 2 independent parts, one for each index of `group`. The reference program is written for one: setup_inputs(seed, part) draws one part's arguments, and reference() takes and returns one part's arrays. A program takes and returns all parts, laid end to end along the dimension named above; each array names one. Nothing has to cross between parts.
All inputs are finite; a program needn't handle non-finite values.
Results may differ from the reference program's by a relative error of at most 0.0065.
Values may be sent and summed in bfloat16 or wider, within the bound.
No kernel may reach another device: no remote copies, remote signals or barrier semaphores. Data moves between devices by JAX's collectives and lax.ppermute only.
A program may use at most 128 MiB of HBM per device.

```python
import jax
import jax.numpy as jnp
from jax import lax

HEADS = 12
HEAD = 128
TXT = 256
TOK_DEV = 48
IMG = 768
HD = 1536
N_PATCH = 8


def region_offsets(key, rows, region, width, scale):
    table = jax.random.truncated_normal(key, -4.0, 4.0, (rows // region, width), jnp.float32) * scale
    return jnp.repeat(table, region, axis=0)


def fresh_block(key):
    key_q = jax.random.fold_in(key, 0)
    key_k = jax.random.fold_in(key, 1)
    key_v = jax.random.fold_in(key, 2)
    key_o = jax.random.fold_in(key, 4)
    queries = jax.random.truncated_normal(key_q, -5.0, 5.0, (IMG, HD), jnp.float32)
    keys_rows = jax.random.truncated_normal(key_k, -5.0, 5.0, (IMG, HD), jnp.float32)
    values = jax.random.truncated_normal(key_v, -5.0, 5.0, (IMG, HD), jnp.float32)
    values = values + region_offsets(key_o, IMG, 2 * TOK_DEV, HD, 3.0)
    return jnp.stack([queries, keys_rows, values]).astype(jnp.bfloat16)


def draw_fresh_first(key, part):
    key = jax.random.fold_in(key, 1)
    return fresh_block(key)


def draw_fresh_second(key, part):
    key = jax.random.fold_in(key, 2)
    return fresh_block(key)


def draw_stale_cache(key, part):
    key = jax.random.fold_in(key, 3)
    key_k, key_v, key_o = jax.random.split(key, 3)
    values = jax.random.truncated_normal(key_v, -5.0, 5.0, (IMG, HD), jnp.float32)
    keys_rows = jax.random.truncated_normal(key_k, -5.0, 5.0, (IMG, HD), jnp.float32)
    values = values + region_offsets(key_o, IMG, 2 * TOK_DEV, HD, 3.0)
    return jnp.stack([keys_rows, values]).astype(jnp.bfloat16)


def text_block(key):
    key_k, key_v, key_o = jax.random.split(key, 3)
    values = jax.random.truncated_normal(key_v, -5.0, 5.0, (TXT, HD), jnp.float32)
    keys_rows = jax.random.truncated_normal(key_k, -5.0, 5.0, (TXT, HD), jnp.float32)
    values = values + region_offsets(key_o, TXT, TXT, HD, 3.0)
    return jnp.stack([keys_rows, values]).astype(jnp.bfloat16)


def draw_text_first(key, part):
    key = jax.random.fold_in(key, 4)
    return text_block(key)


def draw_text_second(key, part):
    key = jax.random.fold_in(key, 5)
    return text_block(key)


def touch_ends(entries, key, smallest, largest):
    longest = entries.shape.index(max(entries.shape))
    spots = []
    for shift in (0, 1):
        where = [jax.random.randint(jax.random.fold_in(key, axis), (), 0, length) for axis, length in enumerate(entries.shape)]
        where[longest] = (where[longest] + shift) % entries.shape[longest]
        spots.append(tuple(where))
    return entries.at[spots[0]].set(smallest).at[spots[1]].set(largest)


def setup_inputs(seed: int = 0, part: int = 0) -> dict:
    seeds = jax.random.split(jax.random.key(seed), 7)
    part_keys = jax.random.split(jax.random.fold_in(seeds[6], part), 7)
    return {
        "fresh_first": draw_fresh_first(jax.random.fold_in(jax.random.fold_in(seeds[6], part), 71), part),
        "fresh_second": draw_fresh_second(jax.random.fold_in(jax.random.fold_in(seeds[6], part), 71), part),
        "stale_cache": draw_stale_cache(jax.random.fold_in(jax.random.fold_in(seeds[6], part), 71), part),
        "stale_exponent": touch_ends(jax.random.randint(part_keys[3], (2, HEADS), -2, 2), jax.random.fold_in(part_keys[3], 1), -2, 1).astype(jnp.int32),
        "text_first": draw_text_first(jax.random.fold_in(jax.random.fold_in(seeds[6], part), 71), part),
        "text_second": draw_text_second(jax.random.fold_in(jax.random.fold_in(seeds[6], part), 71), part),
    }


def split_heads(array):
    return array.reshape(array.shape[0], HEADS, HEAD).transpose(1, 0, 2)


def one_step(fresh, far_keys, far_values, key_scale, value_scale, text):
    queries = split_heads(fresh[0])
    own_keys = split_heads(fresh[1])
    own_values = split_heads(fresh[2])
    far_k = split_heads(far_keys)
    far_v = split_heads(far_values)
    text_k = split_heads(text[0])
    text_v = split_heads(text[1])
    patch_rows = IMG // N_PATCH
    inverse = 1.0 / (HEAD ** 0.5)

    def per_head(items):
        q_head, k_head, v_head, fk_head, fv_head, tk_head, tv_head, k_sc, v_sc = items

        def per_patch(index):
            start = (index * patch_rows).astype(jnp.int32)
            q_rows = lax.dynamic_slice_in_dim(q_head, start, patch_rows, 0)
            k_rows = lax.dynamic_slice_in_dim(k_head, start, patch_rows, 0)
            v_rows = lax.dynamic_slice_in_dim(v_head, start, patch_rows, 0)
            s_own = jnp.dot(q_rows, k_rows.T, preferred_element_type=jnp.float32) * inverse
            s_text = jnp.dot(q_rows, tk_head.T, preferred_element_type=jnp.float32) * inverse
            s_far = jnp.dot(q_rows, fk_head.T, preferred_element_type=jnp.float32) * (k_sc * inverse)
            places = jnp.arange(IMG, dtype=jnp.int32)
            inside = (places >= start) & (places < start + patch_rows)
            s_far = jnp.where(inside[None, :], -jnp.inf, s_far)
            top = jnp.maximum(jnp.maximum(s_own.max(-1), s_text.max(-1)), s_far.max(-1))
            w_own = jnp.exp(s_own - top[:, None])
            w_text = jnp.exp(s_text - top[:, None])
            w_far = jnp.exp(s_far - top[:, None])
            total = w_own.sum(-1) + w_text.sum(-1) + w_far.sum(-1)
            numer = jnp.dot(w_own.astype(jnp.bfloat16), v_rows, preferred_element_type=jnp.float32)
            numer = numer + jnp.dot(w_text.astype(jnp.bfloat16), tv_head, preferred_element_type=jnp.float32)
            numer = numer + jnp.dot(w_far.astype(jnp.bfloat16), fv_head, preferred_element_type=jnp.float32) * v_sc
            return numer / total[:, None]

        blocks = lax.map(per_patch, jnp.arange(N_PATCH, dtype=jnp.int32))
        return blocks.reshape(IMG, HEAD)

    result = lax.map(per_head, (queries, own_keys, own_values, far_k, far_v, text_k, text_v, key_scale, value_scale))
    return result.transpose(1, 0, 2).reshape(IMG, HEADS * HEAD).astype(jnp.bfloat16)


def reference(fresh_first, fresh_second, stale_cache, stale_exponent, text_first, text_second):
    key_scale = jnp.exp2(stale_exponent[0].astype(jnp.float32))
    value_scale = jnp.exp2(stale_exponent[1].astype(jnp.float32))
    attended_first = one_step(fresh_first, stale_cache[0], stale_cache[1], key_scale, value_scale, text_first)
    unit = jnp.ones((HEADS,), jnp.float32)
    attended_second = one_step(fresh_second, fresh_first[1], fresh_first[2], unit, unit, text_second)
    return attended_first, attended_second
```

```python
import functools

import jax
import jax.numpy as jnp
from jax import lax
from jax.experimental import pallas as pl
from jax.experimental.pallas import tpu as pltpu
from jax.sharding import PartitionSpec as P

HEAD = 128
COLUMNS = 2
BF16 = jnp.bfloat16
F32 = jnp.float32


def heads_view(array):
    return array.reshape(array.shape[0], array.shape[1] // HEAD, HEAD)


def absorb(carry, queries, keys_rows, values, key_scale, value_scale, keep):
    top, total, accum = carry
    inverse = 1.0 / HEAD**0.5
    score = jnp.einsum("qhd,khd->hqk", queries, keys_rows, preferred_element_type=F32)
    score = score * (key_scale * inverse)[:, None, None]
    if keep is not None:
        score = jnp.where(keep[None, None, :], score, -jnp.inf)
    new_top = jnp.maximum(top, score.max(-1))
    fade = jnp.exp(top - new_top)
    weight = jnp.exp(score - new_top[:, :, None])
    total = total * fade + weight.sum(-1)
    addend = jnp.einsum("hqk,khd->qhd", weight.astype(BF16), values, preferred_element_type=F32)
    accum = accum * fade.T[:, :, None] + addend * value_scale[None, :, None]
    return (new_top, total, accum)


def general_step(mine, text, far, keep, key_scale, value_scale):
    queries = heads_view(mine[0])
    rows, local_heads = queries.shape[:2]
    unit = jnp.ones((local_heads,), F32)
    carry = (
        jnp.full((local_heads, rows), -jnp.inf, F32),
        jnp.zeros((local_heads, rows), F32),
        jnp.zeros((rows, local_heads, HEAD), F32),
    )
    carry = absorb(carry, queries, heads_view(text[0]), heads_view(text[1]), unit, unit, None)
    carry = absorb(carry, queries, heads_view(mine[1]), heads_view(mine[2]), unit, unit, None)
    carry = absorb(carry, queries, heads_view(far[0]), heads_view(far[1]), key_scale, value_scale, keep)
    top, total, accum = carry
    result = (accum / total.T[:, :, None]).reshape(rows, local_heads * HEAD).astype(BF16)
    return lax.all_to_all(result, "uly", split_axis=0, concat_axis=1, tiled=True)


def general_shards(fresh_first, fresh_second, stale_cache, stale_exponent, text_first, text_second):
    local_heads = stale_exponent.shape[1] // lax.axis_size("uly")
    first_head = lax.axis_index("uly") * local_heads
    exponents = lax.dynamic_slice_in_dim(stale_exponent, first_head, local_heads, 1)
    scales = jnp.exp2(exponents.astype(F32))
    unit = jnp.ones((local_heads,), F32)
    mine_first = lax.all_to_all(fresh_first, "uly", split_axis=2, concat_axis=1, tiled=True)
    mine_second = lax.all_to_all(fresh_second, "uly", split_axis=2, concat_axis=1, tiled=True)
    rows = mine_first.shape[1]
    own_start = lax.axis_index("patch") * rows
    stale = lax.all_gather(stale_cache, "patch", axis=1, tiled=True)
    refreshed = lax.all_gather(mine_first[1:], "patch", axis=1, tiled=True)
    places = jnp.arange(stale.shape[1], dtype=jnp.int32)
    keep = (places < own_start) | (places >= own_start + rows)
    return (
        general_step(mine_first, text_first, stale, keep, scales[0], scales[1]),
        general_step(mine_second, text_second, refreshed, keep, unit, unit),
    )


def attention_kernel(scale_ref, q_ref, tk_ref, tv_ref, ok_ref, ov_ref, *rest, rows):
    fk_refs, fv_refs, out_ref = rest[0:4], rest[4:8], rest[8]
    head = pl.program_id(0)
    inverse = 1.0 / HEAD**0.5
    key_factor = scale_ref[0, head] * inverse
    value_factor = scale_ref[1, head]

    def dot_t(a, b):
        return lax.dot_general(a, b, (((1,), (1,)), ((), ())), preferred_element_type=F32)

    def dot(a, b):
        return jnp.dot(a, b, preferred_element_type=F32)

    q = q_ref[...]
    count = q.shape[0]
    block = lax.broadcasted_iota(jnp.int32, (count, count), 0) // rows
    inside = block == lax.broadcasted_iota(jnp.int32, (count, count), 1) // rows
    text = dot_t(q, tk_ref[...]) * inverse
    near = [
        jnp.where(inside, dot_t(q, ok_ref[i]) * inverse, dot_t(q, fk_refs[i][...]) * key_factor)
        for i in range(2)
    ]
    away = [dot_t(q, fk_refs[i][...]) * key_factor for i in range(2, 4)]
    scores = [text] + near + away
    top = functools.reduce(jnp.maximum, [s.max(-1, keepdims=True) for s in scores])
    weights = [jnp.exp(s - top) for s in scores]
    total = functools.reduce(jnp.add, [w.sum(-1, keepdims=True) for w in weights])
    rounded = [w.astype(BF16) for w in weights]
    zero = jnp.zeros((), BF16)
    own = dot(rounded[0], tv_ref[...])
    for i in range(2):
        own = own + dot(jnp.where(inside, rounded[1 + i], zero), ov_ref[i])
    far = dot(rounded[3], fv_refs[2][...]) + dot(rounded[4], fv_refs[3][...])
    for i in range(2):
        far = far + dot(jnp.where(inside, zero, rounded[1 + i]), fv_refs[i][...])
    out_ref[...] = ((own + value_factor * far) / total).astype(BF16)


def attention(scales, q, text, own_keys, own_values, far_keys, far_values, rows):
    count, width = q.shape
    heads = width // HEAD
    text_rows = text.shape[1]
    flat = pl.BlockSpec((count, HEAD), lambda h: (0, h))
    pair = pl.BlockSpec((2, count, HEAD), lambda h: (0, 0, h))
    text_spec = pl.BlockSpec((text_rows, HEAD), lambda h: (0, h))
    keys = text_rows + 4 * count
    return pl.pallas_call(
        functools.partial(attention_kernel, rows=rows),
        grid=(heads,),
        out_shape=jax.ShapeDtypeStruct((count, width), BF16),
        in_specs=[pl.BlockSpec(memory_space=pltpu.SMEM), flat, text_spec, text_spec, pair, pair] + [flat] * 8,
        out_specs=flat,
        cost_estimate=pl.CostEstimate(
            flops=4 * count * keys * width, bytes_accessed=2 * width * (2 * keys + 4 * count), transcendentals=count * keys * heads
        ),
    )(scales, q, text[0], text[1], own_keys, own_values, *far_keys, *far_values)


def layered_shards(layers, fresh_first, fresh_second, stale_cache, stale_exponent, text_first, text_second):
    core = lax.axis_index("uly")
    patch = lax.axis_index("patch")
    layer = patch // COLUMNS
    rows, features = fresh_first.shape[1:]
    width = features // layers
    heads = width // HEAD
    half = features // 2

    def layer_shift(x, shift):
        pairs = [
            (z * COLUMNS + y, (z + shift) % layers * COLUMNS + y) for z in range(layers) for y in range(COLUMNS)
        ]
        return lax.ppermute(x, "patch", pairs)

    def other_column(x):
        return lax.ppermute(x, "patch", [(p, p ^ 1) for p in range(layers * COLUMNS)])

    def other_core(x):
        return lax.ppermute(x, "uly", [(0, 1), (1, 0)])

    def columns_of(x, shift):
        start = (layer + shift) % layers * width
        return lax.dynamic_slice_in_dim(x, start, width, x.ndim - 1)

    keep = lax.dynamic_slice_in_dim(stale_cache, core * rows, rows, 1)
    give = lax.dynamic_slice_in_dim(stale_cache, (1 - core) * rows, rows, 1)
    got = other_core(give)
    stale = jnp.where(core == 0, jnp.concatenate([keep, got], 2), jnp.concatenate([got, keep], 2))

    source = jnp.concatenate([stale, fresh_first[1:]], 0)
    pieces = [columns_of(source, 0)] + [layer_shift(columns_of(source, s), s) for s in range(1, layers)]
    later = jnp.concatenate([fresh_first[:1], fresh_second], 0)
    later = [columns_of(later, 0)] + [layer_shift(columns_of(later, s), s) for s in range(1, layers)]

    count = layers * rows
    here = jnp.concatenate(pieces, 1)
    there = other_column(here)
    here_twin = other_core(here)
    there_twin = other_core(there)
    later = jnp.concatenate(later, 1)
    second_twin = other_core(later[2:])

    text = jnp.concatenate([text_first, text_second], 0)
    text = lax.dynamic_slice_in_dim(text, layer * width % half, width, 2)
    text = jnp.where(core == layer * width // half, text, other_core(text))

    scales = jnp.exp2(lax.dynamic_slice_in_dim(stale_exponent, layer * heads, heads, 1).astype(F32))
    far = [here, here_twin, there, there_twin]
    first = attention(
        scales,
        later[0],
        text[:2],
        jnp.stack([here[2], here_twin[2]]),
        jnp.stack([here[3], here_twin[3]]),
        [f[0] for f in far],
        [f[1] for f in far],
        rows,
    )
    second = attention(
        jnp.ones_like(scales),
        later[1],
        text[2:],
        jnp.stack([later[2], second_twin[0]]),
        jnp.stack([later[3], second_twin[1]]),
        [f[2] for f in far],
        [f[3] for f in far],
        rows,
    )

    def back(result):
        blocks = result.reshape(layers, rows, width)
        out = jnp.zeros((rows, features), BF16)
        for s in range(layers):
            block = blocks[s] if s == 0 else layer_shift(blocks[s], -s)
            out = lax.dynamic_update_slice_in_dim(out, block, (layer + s) % layers * width, 1)
        return out

    return back(first), back(second)


def solution(mesh):
    placed = (
        P(None, ("group", "patch", "uly"), None),
        P(None, ("group", "patch", "uly"), None),
        P(None, ("group", "patch"), "uly"),
        P("group", None),
        P(None, "group", "uly"),
        P(None, "group", "uly"),
    )

    def shards(*arrays):
        layers = mesh.shape["patch"] // COLUMNS
        heads = arrays[0].shape[2] // HEAD
        if mesh.shape["uly"] == 2 and layers % 2 == 0 and heads % layers == 0:
            return layered_shards(layers, *arrays)
        return general_shards(*arrays)

    return jax.shard_map(
        shards,
        mesh=mesh,
        in_specs=placed,
        out_specs=(P(("group", "patch", "uly"), None), P(("group", "patch", "uly"), None)),
        check_vma=False,
    )
```

```python
import functools

import jax
import jax.numpy as jnp
from jax import lax
from jax.experimental import pallas as pl
from jax.experimental.pallas import tpu as pltpu
from jax.sharding import PartitionSpec as P

HEAD = 128
COLUMNS = 2
BF16 = jnp.bfloat16
F32 = jnp.float32


def heads_view(array):
    return array.reshape(array.shape[0], array.shape[1] // HEAD, HEAD)


def absorb(carry, queries, keys_rows, values, key_scale, value_scale, keep):
    top, total, accum = carry
    inverse = 1.0 / HEAD**0.5
    score = jnp.einsum("qhd,khd->hqk", queries, keys_rows, preferred_element_type=F32)
    score = score * (key_scale * inverse)[:, None, None]
    if keep is not None:
        score = jnp.where(keep[None, None, :], score, -jnp.inf)
    new_top = jnp.maximum(top, score.max(-1))
    fade = jnp.exp(top - new_top)
    weight = jnp.exp(score - new_top[:, :, None])
    total = total * fade + weight.sum(-1)
    addend = jnp.einsum("hqk,khd->qhd", weight.astype(BF16), values, preferred_element_type=F32)
    accum = accum * fade.T[:, :, None] + addend * value_scale[None, :, None]
    return (new_top, total, accum)


def general_step(mine, text, far, keep, key_scale, value_scale):
    queries = heads_view(mine[0])
    rows, local_heads = queries.shape[:2]
    unit = jnp.ones((local_heads,), F32)
    carry = (
        jnp.full((local_heads, rows), -jnp.inf, F32),
        jnp.zeros((local_heads, rows), F32),
        jnp.zeros((rows, local_heads, HEAD), F32),
    )
    carry = absorb(carry, queries, heads_view(text[0]), heads_view(text[1]), unit, unit, None)
    carry = absorb(carry, queries, heads_view(mine[1]), heads_view(mine[2]), unit, unit, None)
    carry = absorb(carry, queries, heads_view(far[0]), heads_view(far[1]), key_scale, value_scale, keep)
    top, total, accum = carry
    result = (accum / total.T[:, :, None]).reshape(rows, local_heads * HEAD).astype(BF16)
    return lax.all_to_all(result, "uly", split_axis=0, concat_axis=1, tiled=True)


def general_shards(fresh_first, fresh_second, stale_cache, stale_exponent, text_first, text_second):
    local_heads = stale_exponent.shape[1] // lax.axis_size("uly")
    first_head = lax.axis_index("uly") * local_heads
    exponents = lax.dynamic_slice_in_dim(stale_exponent, first_head, local_heads, 1)
    scales = jnp.exp2(exponents.astype(F32))
    unit = jnp.ones((local_heads,), F32)
    mine_first = lax.all_to_all(fresh_first, "uly", split_axis=2, concat_axis=1, tiled=True)
    mine_second = lax.all_to_all(fresh_second, "uly", split_axis=2, concat_axis=1, tiled=True)
    rows = mine_first.shape[1]
    own_start = lax.axis_index("patch") * rows
    stale = lax.all_gather(stale_cache, "patch", axis=1, tiled=True)
    refreshed = lax.all_gather(mine_first[1:], "patch", axis=1, tiled=True)
    places = jnp.arange(stale.shape[1], dtype=jnp.int32)
    keep = (places < own_start) | (places >= own_start + rows)
    return (
        general_step(mine_first, text_first, stale, keep, scales[0], scales[1]),
        general_step(mine_second, text_second, refreshed, keep, unit, unit),
    )


def dot_t(a, b):
    return lax.dot_general(a, b, (((1,), (1,)), ((), ())), preferred_element_type=F32)


def dot(a, b):
    return jnp.dot(a, b, preferred_element_type=F32)


def attend(q, text, own, near, away, inside, key_factor, value_factor):
    inverse = 1.0 / HEAD**0.5
    scores = [
        dot_t(q, text[0]) * inverse,
        jnp.where(inside, dot_t(q, own[0]) * inverse, dot_t(q, near[0]) * key_factor),
        dot_t(q, away[0]) * key_factor,
    ]
    top = functools.reduce(jnp.maximum, [s.max(-1, keepdims=True) for s in scores])
    weights = [jnp.exp(s - top) for s in scores]
    total = functools.reduce(jnp.add, [w.sum(-1, keepdims=True) for w in weights])
    w_text, w_near, w_away = [w.astype(BF16) for w in weights]
    zero = jnp.zeros((), BF16)
    kept = dot(w_text, text[1]) + dot(jnp.where(inside, w_near, zero), own[1])
    far = dot(jnp.where(inside, zero, w_near), near[1]) + dot(w_away, away[1])
    return (kept + value_factor * far) / total


def store_blocks(out_refs, result, lanes):
    rows = out_refs[0].shape[0]
    for i, out_ref in enumerate(out_refs):
        out_ref[:, lanes] = result[i * rows : (i + 1) * rows].astype(BF16)


def first_kernel(scale_ref, order_ref, q_ref, text_ref, own_ref, twin_ref, near_ref, other_ref, away_ref, away_twin_ref, *out_refs):
    count, width = q_ref.shape
    layers, rows = len(out_refs), out_refs[0].shape[0]
    shape = (count, 2 * count)
    inside = (
        lax.broadcasted_iota(jnp.int32, shape, 0) // rows == lax.broadcasted_iota(jnp.int32, shape, 1) // (2 * rows)
    )
    for head in range(width // HEAD):
        lanes = slice(head * HEAD, (head + 1) * HEAD)

        def own(i):
            cut = [slice(s * rows, (s + 1) * rows) for s in range(layers)]
            return jnp.concatenate([r[i, c, lanes] for c in cut for r in (own_ref, twin_ref)], 0)

        def near(i):
            blocks = []
            for s in range(layers):
                place = order_ref[1, s]
                mine, other = near_ref[place, i, :, lanes], other_ref[place, i, :, lanes]
                blocks.append(jnp.where(order_ref[0, s] == 0, mine, other))
            return jnp.concatenate(blocks, 0)

        def away(i):
            return jnp.concatenate([r[k, i, :, lanes] for r in (away_ref, away_twin_ref) for k in range(layers // 2)], 0)

        result = attend(
            q_ref[:, lanes],
            (text_ref[0, :, lanes], text_ref[1, :, lanes]),
            (own(0), own(1)),
            (near(0), near(1)),
            (away(0), away(1)),
            inside,
            scale_ref[0, head] * (1.0 / HEAD**0.5),
            scale_ref[1, head],
        )
        store_blocks(out_refs, result, lanes)


def second_kernel(q_ref, text_ref, own_ref, own_twin_ref, near_ref, near_twin_ref, away_ref, away_twin_ref, *out_refs):
    count, width = q_ref.shape
    rows = out_refs[0].shape[0]
    shape = (count, 2 * count)
    inside = (
        lax.broadcasted_iota(jnp.int32, shape, 0) // rows
        == lax.broadcasted_iota(jnp.int32, shape, 1) % count // rows
    )
    for head in range(width // HEAD):
        lanes = slice(head * HEAD, (head + 1) * HEAD)

        def pair(a, b):
            return tuple(jnp.concatenate([a[i, :, lanes], b[i, :, lanes]], 0) for i in range(2))

        result = attend(
            q_ref[:, lanes],
            (text_ref[2, :, lanes], text_ref[3, :, lanes]),
            pair(own_ref, own_twin_ref),
            pair(near_ref, near_twin_ref),
            pair(away_ref, away_twin_ref),
            inside,
            1.0 / HEAD**0.5,
            1.0,
        )
        store_blocks(out_refs, result, lanes)


def call_attention(kernel, layers, scalars, q, text, *others):
    count, width = q.shape
    keys = text.shape[1] + 4 * count
    in_vmem = pl.BlockSpec(memory_space=pltpu.VMEM)
    return pl.pallas_call(
        kernel,
        out_shape=[jax.ShapeDtypeStruct((count // layers, width), BF16)] * layers,
        in_specs=[pl.BlockSpec(memory_space=pltpu.SMEM)] * len(scalars) + [in_vmem] * (2 + len(others)),
        out_specs=[in_vmem] * layers,
        compiler_params=pltpu.CompilerParams(vmem_limit_bytes=32 * 1024 * 1024),
        cost_estimate=pl.CostEstimate(
            flops=4 * count * keys * width, bytes_accessed=4 * width * (keys + count), transcendentals=count * keys * width // HEAD
        ),
    )(*scalars, q, text, *others)


def layered_shards(layers, fresh_first, fresh_second, stale_cache, stale_exponent, text_first, text_second):
    core = lax.axis_index("uly")
    layer = lax.axis_index("patch") // COLUMNS
    rows, features = fresh_first.shape[1:]
    width = features // layers
    heads = width // HEAD
    half = features // 2
    rounds = layers // 2

    def layer_shift(x, shift):
        pairs = [
            (z * COLUMNS + y, (z + shift) % layers * COLUMNS + y) for z in range(layers) for y in range(COLUMNS)
        ]
        return lax.ppermute(x, "patch", pairs)

    def stale_round(x, k):
        pairs = []
        for z in range(layers):
            for y in range(COLUMNS):
                for u in range(2):
                    to = (u * rounds + (z + k) % rounds) * COLUMNS + y
                    pairs.append(((z * COLUMNS + y) * 2 + u, to * 2 + z // rounds))
        return lax.ppermute(x, ("patch", "uly"), pairs)

    def other_column(x):
        return lax.ppermute(x, "patch", [(p, p ^ 1) for p in range(layers * COLUMNS)])

    def other_core(x):
        return lax.ppermute(x, "uly", [(0, 1), (1, 0)])

    def columns_of(x, index):
        return lax.dynamic_slice_in_dim(x, index * width, width, x.ndim - 1)

    def over_layers(x):
        sends = [columns_of(x, (layer + s) % layers) for s in range(layers)]
        return sends[:1] + [layer_shift(sends[s], s) for s in range(1, layers)]

    stale = jnp.stack([stale_round(columns_of(stale_cache, (layer + k) % rounds), k) for k in range(rounds)])
    stale_away = other_column(stale)
    stale_twin = other_core(stale)
    stale_away_twin = other_core(stale_away)
    source = [(layer - s) % layers for s in range(layers)]
    order = jnp.stack(
        [jnp.stack([(L // rounds != core).astype(jnp.int32) for L in source]), jnp.stack([(L - layer) % rounds for L in source])]
    )

    first = over_layers(fresh_first)
    query_first = jnp.concatenate([p[0] for p in first], 0)
    fresh = jnp.concatenate([p[1:] for p in first], 1)
    fresh_away = other_column(fresh)
    fresh_twin = other_core(fresh)
    fresh_away_twin = other_core(fresh_away)

    second = over_layers(fresh_second)
    query_second = jnp.concatenate([p[0] for p in second], 0)
    last = jnp.concatenate([p[1:] for p in second], 1)
    last_twin = other_core(last)

    text = jnp.concatenate([text_first, text_second], 0)
    text = lax.dynamic_slice_in_dim(text, layer * width % half, width, 2)
    text = jnp.where(core == layer * width // half, text, other_core(text))

    scales = jnp.exp2(lax.dynamic_slice_in_dim(stale_exponent, layer * heads, heads, 1).astype(F32))
    first_blocks = call_attention(
        first_kernel, layers, [scales, order], query_first, text, fresh, fresh_twin, stale, stale_twin, stale_away, stale_away_twin
    )
    second_blocks = call_attention(
        second_kernel, layers, [], query_second, text, last, last_twin, fresh, fresh_twin, fresh_away, fresh_away_twin
    )

    def back(blocks):
        out = jnp.zeros((rows, features), BF16)
        for s in range(layers):
            block = blocks[s] if s == 0 else layer_shift(blocks[s], -s)
            out = lax.dynamic_update_slice_in_dim(out, block, (layer + s) % layers * width, 1)
        return out

    return back(first_blocks), back(second_blocks)


def solution(mesh):
    placed = (
        P(None, ("group", "patch", "uly"), None),
        P(None, ("group", "patch", "uly"), None),
        P(None, ("group", "patch"), "uly"),
        P("group", None),
        P(None, "group", "uly"),
        P(None, "group", "uly"),
    )

    def shards(*arrays):
        layers = mesh.shape["patch"] // COLUMNS
        heads = arrays[0].shape[2] // HEAD
        if mesh.shape["uly"] == 2 and layers % 2 == 0 and heads % layers == 0:
            return layered_shards(layers, *arrays)
        return general_shards(*arrays)

    return jax.shard_map(
        shards,
        mesh=mesh,
        in_specs=placed,
        out_specs=(P(("group", "patch", "uly"), None), P(("group", "patch", "uly"), None)),
        check_vma=False,
    )
```

```python
import functools

import jax
import jax.numpy as jnp
from jax import lax
from jax.experimental import pallas as pl
from jax.experimental.pallas import tpu as pltpu
from jax.sharding import PartitionSpec as P

HEAD = 128
COLUMNS = 2
BF16 = jnp.bfloat16
F32 = jnp.float32


def heads_view(array):
    return array.reshape(array.shape[0], array.shape[1] // HEAD, HEAD)


def absorb(carry, queries, keys_rows, values, key_scale, value_scale, keep):
    top, total, accum = carry
    inverse = 1.0 / HEAD**0.5
    score = jnp.einsum("qhd,khd->hqk", queries, keys_rows, preferred_element_type=F32)
    score = score * (key_scale * inverse)[:, None, None]
    if keep is not None:
        score = jnp.where(keep[None, None, :], score, -jnp.inf)
    new_top = jnp.maximum(top, score.max(-1))
    fade = jnp.exp(top - new_top)
    weight = jnp.exp(score - new_top[:, :, None])
    total = total * fade + weight.sum(-1)
    addend = jnp.einsum("hqk,khd->qhd", weight.astype(BF16), values, preferred_element_type=F32)
    accum = accum * fade.T[:, :, None] + addend * value_scale[None, :, None]
    return (new_top, total, accum)


def general_step(mine, text, far, keep, key_scale, value_scale):
    queries = heads_view(mine[0])
    rows, local_heads = queries.shape[:2]
    unit = jnp.ones((local_heads,), F32)
    carry = (
        jnp.full((local_heads, rows), -jnp.inf, F32),
        jnp.zeros((local_heads, rows), F32),
        jnp.zeros((rows, local_heads, HEAD), F32),
    )
    carry = absorb(carry, queries, heads_view(text[0]), heads_view(text[1]), unit, unit, None)
    carry = absorb(carry, queries, heads_view(mine[1]), heads_view(mine[2]), unit, unit, None)
    carry = absorb(carry, queries, heads_view(far[0]), heads_view(far[1]), key_scale, value_scale, keep)
    top, total, accum = carry
    result = (accum / total.T[:, :, None]).reshape(rows, local_heads * HEAD).astype(BF16)
    return lax.all_to_all(result, "uly", split_axis=0, concat_axis=1, tiled=True)


def general_shards(fresh_first, fresh_second, stale_cache, stale_exponent, text_first, text_second):
    local_heads = stale_exponent.shape[1] // lax.axis_size("uly")
    first_head = lax.axis_index("uly") * local_heads
    exponents = lax.dynamic_slice_in_dim(stale_exponent, first_head, local_heads, 1)
    scales = jnp.exp2(exponents.astype(F32))
    unit = jnp.ones((local_heads,), F32)
    mine_first = lax.all_to_all(fresh_first, "uly", split_axis=2, concat_axis=1, tiled=True)
    mine_second = lax.all_to_all(fresh_second, "uly", split_axis=2, concat_axis=1, tiled=True)
    rows = mine_first.shape[1]
    own_start = lax.axis_index("patch") * rows
    stale = lax.all_gather(stale_cache, "patch", axis=1, tiled=True)
    refreshed = lax.all_gather(mine_first[1:], "patch", axis=1, tiled=True)
    places = jnp.arange(stale.shape[1], dtype=jnp.int32)
    keep = (places < own_start) | (places >= own_start + rows)
    return (
        general_step(mine_first, text_first, stale, keep, scales[0], scales[1]),
        general_step(mine_second, text_second, refreshed, keep, unit, unit),
    )


def dot_t(a, b):
    return lax.dot_general(a, b, (((1,), (1,)), ((), ())), preferred_element_type=F32)


def dot(a, b):
    return jnp.dot(a, b, preferred_element_type=F32)


def attend(q, text, own, near, away, inside, key_factor, value_factor):
    inverse = 1.0 / HEAD**0.5
    scores = [
        dot_t(q, text[0]) * inverse,
        jnp.where(inside, dot_t(q, own[0]) * inverse, dot_t(q, near[0]) * key_factor),
        dot_t(q, away[0]) * key_factor,
    ]
    top = functools.reduce(jnp.maximum, [s.max(-1, keepdims=True) for s in scores])
    weights = [jnp.exp(s - top) for s in scores]
    total = functools.reduce(jnp.add, [w.sum(-1, keepdims=True) for w in weights])
    w_text, w_near, w_away = [w.astype(BF16) for w in weights]
    zero = jnp.zeros((), BF16)
    kept = dot(w_text, text[1]) + dot(jnp.where(inside, w_near, zero), own[1])
    far = dot(jnp.where(inside, zero, w_near), near[1]) + dot(w_away, away[1])
    return (kept + value_factor * far) / total


def store_blocks(out_refs, result, lanes):
    rows = out_refs[0].shape[0]
    for i, out_ref in enumerate(out_refs):
        out_ref[:, lanes] = result[i * rows : (i + 1) * rows].astype(BF16)


def kernel_columns(ref, index):
    width = index[1]
    return ref.at[..., pl.ds(pl.multiple_of(index[0] * width, width), width)]


def run_copies(copies, sems):
    started = [pltpu.make_async_copy(a, b, sems.at[i]) for i, (a, b) in enumerate(copies)]
    for c in started:
        c.start()
    for c in started:
        c.wait()


def pack_shared_kernel(stale_ref, first_ref, *refs, layers):
    rounds = layers // 2
    layer = lax.axis_index("patch") // COLUMNS
    out_refs, sems = refs[:-1], refs[-1]
    width = out_refs[0].shape[-1]
    copies = [
        (kernel_columns(stale_ref, ((layer + k) % rounds, width)), out_refs[k]) for k in range(rounds)
    ]
    for s in range(layers):
        copies.append((kernel_columns(first_ref.at[1:], ((layer + s) % layers, width)), out_refs[rounds + s]))
    run_copies(copies, sems)


def pack_owned_kernel(first_ref, second_ref, text_first_ref, text_second_ref, *refs, layers):
    layer = lax.axis_index("patch") // COLUMNS
    out_refs, text_ref, sems = refs[:-2], refs[-2], refs[-1]
    width = text_ref.shape[-1]
    copies = []
    for s, out_ref in enumerate(out_refs):
        copies.append((kernel_columns(first_ref.at[:1], ((layer + s) % layers, width)), out_ref.at[:1]))
        copies.append((kernel_columns(second_ref, ((layer + s) % layers, width)), out_ref.at[1:]))
    for i, ref in enumerate((text_first_ref, text_second_ref)):
        copies.append((kernel_columns(ref, (layer % (layers // 2), width)), text_ref.at[2 * i : 2 * i + 2]))
    run_copies(copies, sems)


def pack(kernel, shapes, copies, *operands):
    return pl.pallas_call(
        kernel,
        out_shape=[jax.ShapeDtypeStruct(shape, BF16) for shape in shapes],
        in_specs=[pl.BlockSpec(memory_space=pl.ANY)] * len(operands),
        out_specs=[pl.BlockSpec(memory_space=pltpu.VMEM)] * len(shapes),
        scratch_shapes=[pltpu.SemaphoreType.DMA((copies,))],
        cost_estimate=pl.CostEstimate(flops=0, bytes_accessed=1 << 20, transcendentals=0),
    )(*operands)


def both_kernel(scale_ref, order_ref, queries_ref, text_ref, text_twin_ref, last_ref, last_twin_ref, *refs, parts):
    sets, refs = [], list(refs)
    for p in parts:
        sets.append(refs[:p])
        refs = refs[p:]
    near_sets, away_sets = sets[:2], sets[2:]
    out_refs = refs
    layers = len(out_refs)
    rounds = layers // 2
    count, width = queries_ref.shape[1:]
    rows = count // layers
    inverse = 1.0 / HEAD**0.5
    shape = (count, 2 * count)
    query_block = lax.broadcasted_iota(jnp.int32, shape, 0) // rows
    place = lax.broadcasted_iota(jnp.int32, shape, 1)
    inside = [query_block == place // (2 * rows), query_block == place % count // rows]

    def fresh_view(pieces):
        return (pieces[1], 0) if len(pieces) == 2 else (pieces[0], layers)

    for step in range(2):
        for head in range(width // HEAD):
            lanes = slice(head * HEAD, (head + 1) * HEAD)

            def text(i):
                at = 2 * step + i
                return jnp.where(order_ref[2, 0] == 0, text_ref[at, :, lanes], text_twin_ref[at, :, lanes])

            def fresh(pieces, i):
                ref, base = fresh_view(pieces)
                half = layers // 2
                return jnp.concatenate([ref[base + half * i + j, :, lanes] for j in range(half)], 0)

            def fresh_all(pair, i):
                return jnp.concatenate([fresh(p, i) for p in pair], 0)

            def in_patches(i):
                own, twin = (fresh(p, i) for p in near_sets)
                return jnp.concatenate([x[s * rows : (s + 1) * rows] for s in range(layers) for x in (own, twin)], 0)

            def last(i):
                return jnp.concatenate([last_ref[2 + i, :, lanes], last_twin_ref[last_twin_ref.shape[0] - 2 + i, :, lanes]], 0)

            def stale_in_patches(i):
                blocks = []
                for s in range(layers):
                    at = 2 * order_ref[1, s] + i
                    blocks.append(jnp.where(order_ref[0, s] == 0, *(p[0][at, :, lanes] for p in near_sets)))
                return jnp.concatenate(blocks, 0)

            def stale_elsewhere(i):
                return jnp.concatenate([p[0][2 * k + i, :, lanes] for p in away_sets for k in range(rounds)], 0)

            if step == 0:
                own = [in_patches(i) for i in range(2)]
                near = [stale_in_patches(i) for i in range(2)]
                away = [stale_elsewhere(i) for i in range(2)]
            else:
                own = [last(i) for i in range(2)]
                near = [fresh_all(near_sets, i) for i in range(2)]
                away = [fresh_all(away_sets, i) for i in range(2)]
            result = attend(
                queries_ref[step, :, lanes],
                [text(i) for i in range(2)],
                own,
                near,
                away,
                inside[step],
                inverse if step else scale_ref[0, head] * inverse,
                1.0 if step else scale_ref[1, head],
            )
            for i, out_ref in enumerate(out_refs):
                out_ref[step, :, lanes] = result[i * rows : (i + 1) * rows].astype(BF16)


def call_both(layers, scalars, parts, *operands):
    count, width = operands[0].shape[1:]
    keys = 2 * operands[1].shape[1] + 8 * count
    in_vmem = pl.BlockSpec(memory_space=pltpu.VMEM)
    return pl.pallas_call(
        functools.partial(both_kernel, parts=parts),
        out_shape=[jax.ShapeDtypeStruct((2, count // layers, width), BF16)] * layers,
        in_specs=[pl.BlockSpec(memory_space=pltpu.SMEM)] * len(scalars) + [in_vmem] * len(operands),
        out_specs=[in_vmem] * layers,
        compiler_params=pltpu.CompilerParams(vmem_limit_bytes=32 * 1024 * 1024),
        cost_estimate=pl.CostEstimate(
            flops=4 * count * keys * width, bytes_accessed=4 * width * (keys + count), transcendentals=count * keys * width // HEAD
        ),
    )(*scalars, *operands)


def layered_shards(layers, fresh_first, fresh_second, stale_cache, stale_exponent, text_first, text_second):
    core = lax.axis_index("uly")
    layer = lax.axis_index("patch") // COLUMNS
    rows, features = fresh_first.shape[1:]
    width = features // layers
    heads = width // HEAD
    half = features // 2
    rounds = layers // 2
    count = layers * rows
    text_rows = text_first.shape[1]

    def after(x, *needed):
        return lax.optimization_barrier((x,) + needed)[0]

    def layer_swap(x, shift):
        pairs = [(z * COLUMNS + y, (z + shift) % layers * COLUMNS + y) for z in range(layers) for y in range(COLUMNS)]
        return x if shift == 0 else lax.ppermute(x, "patch", pairs)

    def stale_round(x, k):
        pairs = []
        for z in range(layers):
            for y in range(COLUMNS):
                for u in range(2):
                    to = (u * rounds + (z + k) % rounds) * COLUMNS + y
                    pairs.append(((z * COLUMNS + y) * 2 + u, to * 2 + z // rounds))
        return lax.ppermute(x, ("patch", "uly"), pairs)

    def other_column(x):
        return lax.ppermute(x, "patch", [(p, p ^ 1) for p in range(layers * COLUMNS)])

    def other_core(x):
        return lax.ppermute(x, "uly", [(0, 1), (1, 0)])

    def columns_of(x, index):
        return lax.dynamic_slice_in_dim(x, index * width, width, x.ndim - 1)

    shared = [columns_of(stale_cache, (layer + k) % rounds) for k in range(rounds)]
    shared += [columns_of(fresh_first[1:], (layer + s) % layers) for s in range(layers)]
    *owned, text = pack(
        functools.partial(pack_owned_kernel, layers=layers),
        [(4, rows, width)] * layers + [(4, text_rows, width)],
        2 * layers + 2,
        after(fresh_first, shared),
        fresh_second,
        text_first,
        text_second,
    )
    stale = [stale_round(shared[k], k) for k in range(rounds)]
    fresh = [layer_swap(shared[rounds + s], s) for s in range(layers)]
    fresh[0] = after(fresh[0], owned)
    fresh_block = jnp.concatenate(fresh, 1).reshape(layers, 2 * rows, width)
    stale_block = jnp.concatenate(stale, 0)
    near = jnp.concatenate([stale_block, fresh_block], 0)
    away = [other_column(near)]
    owned = {s: layer_swap(owned[s], s) for s in (0, 2, 1, 3)}
    owned = [owned[s] for s in range(layers)]
    away_twin = [other_core(away[0][:layers]), other_core(away[0][layers:])]
    last = jnp.concatenate(owned, 1)
    near_twin = [other_core(near)]
    last_twin = other_core(last[2:])
    text_twin = other_core(after(text, owned[1]))
    sets = [[near], near_twin, away, away_twin]

    scales = jnp.exp2(lax.dynamic_slice_in_dim(stale_exponent, layer * heads, heads, 1).astype(F32))
    source = [(layer - s) % layers for s in range(layers)]
    order = jnp.stack(
        [jnp.stack([(L // rounds != core).astype(jnp.int32) for L in source]), jnp.stack([(L - layer) % rounds for L in source]), jnp.full((layers,), (layer // rounds != core).astype(jnp.int32))]
    )
    parts = tuple(len(p) for p in sets)
    flat = [p for pieces in sets for p in pieces]
    blocks = call_both(layers, [scales, order], parts, last[:2], text, text_twin, last, last_twin, *flat)

    out = jnp.zeros((2, rows, features), BF16)
    for s in range(layers):
        out = lax.dynamic_update_slice_in_dim(out, layer_swap(blocks[s], -s), (layer + s) % layers * width, 2)
    return out[0], out[1]


def solution(mesh):
    placed = (
        P(None, ("group", "patch", "uly"), None),
        P(None, ("group", "patch", "uly"), None),
        P(None, ("group", "patch"), "uly"),
        P("group", None),
        P(None, "group", "uly"),
        P(None, "group", "uly"),
    )

    def shards(*arrays):
        layers = mesh.shape["patch"] // COLUMNS
        heads = arrays[0].shape[2] // HEAD
        if mesh.shape["uly"] == 2 and layers == 4 and heads % layers == 0:
            return layered_shards(layers, *arrays)
        return general_shards(*arrays)

    return jax.shard_map(
        shards,
        mesh=mesh,
        in_specs=placed,
        out_specs=(P(("group", "patch", "uly"), None), P(("group", "patch", "uly"), None)),
        check_vma=False,
    )
```

```python
import functools

import jax
import jax.numpy as jnp
from jax import lax
from jax.experimental import pallas as pl
from jax.experimental.pallas import tpu as pltpu
from jax.sharding import PartitionSpec as P

HEAD = 128
LOG2E = 1.4426950408889634
COLUMNS = 2
BF16 = jnp.bfloat16
F32 = jnp.float32


def heads_view(array):
    return array.reshape(array.shape[0], array.shape[1] // HEAD, HEAD)


def absorb(carry, queries, keys_rows, values, key_scale, value_scale, keep):
    top, total, accum = carry
    inverse = 1.0 / HEAD**0.5
    score = jnp.einsum("qhd,khd->hqk", queries, keys_rows, preferred_element_type=F32)
    score = score * (key_scale * inverse)[:, None, None]
    if keep is not None:
        score = jnp.where(keep[None, None, :], score, -jnp.inf)
    new_top = jnp.maximum(top, score.max(-1))
    fade = jnp.exp(top - new_top)
    weight = jnp.exp(score - new_top[:, :, None])
    total = total * fade + weight.sum(-1)
    addend = jnp.einsum("hqk,khd->qhd", weight.astype(BF16), values, preferred_element_type=F32)
    accum = accum * fade.T[:, :, None] + addend * value_scale[None, :, None]
    return (new_top, total, accum)


def general_step(mine, text, far, keep, key_scale, value_scale):
    queries = heads_view(mine[0])
    rows, local_heads = queries.shape[:2]
    unit = jnp.ones((local_heads,), F32)
    carry = (
        jnp.full((local_heads, rows), -jnp.inf, F32),
        jnp.zeros((local_heads, rows), F32),
        jnp.zeros((rows, local_heads, HEAD), F32),
    )
    carry = absorb(carry, queries, heads_view(text[0]), heads_view(text[1]), unit, unit, None)
    carry = absorb(carry, queries, heads_view(mine[1]), heads_view(mine[2]), unit, unit, None)
    carry = absorb(carry, queries, heads_view(far[0]), heads_view(far[1]), key_scale, value_scale, keep)
    top, total, accum = carry
    result = (accum / total.T[:, :, None]).reshape(rows, local_heads * HEAD).astype(BF16)
    return lax.all_to_all(result, "uly", split_axis=0, concat_axis=1, tiled=True)


def general_shards(fresh_first, fresh_second, stale_cache, stale_exponent, text_first, text_second):
    local_heads = stale_exponent.shape[1] // lax.axis_size("uly")
    first_head = lax.axis_index("uly") * local_heads
    exponents = lax.dynamic_slice_in_dim(stale_exponent, first_head, local_heads, 1)
    scales = jnp.exp2(exponents.astype(F32))
    unit = jnp.ones((local_heads,), F32)
    mine_first = lax.all_to_all(fresh_first, "uly", split_axis=2, concat_axis=1, tiled=True)
    mine_second = lax.all_to_all(fresh_second, "uly", split_axis=2, concat_axis=1, tiled=True)
    rows = mine_first.shape[1]
    own_start = lax.axis_index("patch") * rows
    stale = lax.all_gather(stale_cache, "patch", axis=1, tiled=True)
    refreshed = lax.all_gather(mine_first[1:], "patch", axis=1, tiled=True)
    places = jnp.arange(stale.shape[1], dtype=jnp.int32)
    keep = (places < own_start) | (places >= own_start + rows)
    return (
        general_step(mine_first, text_first, stale, keep, scales[0], scales[1]),
        general_step(mine_second, text_second, refreshed, keep, unit, unit),
    )


def dot_t(a, b):
    return lax.dot_general(a, b, (((1,), (1,)), ((), ())), preferred_element_type=F32)


def dot(a, b):
    return jnp.dot(a, b, preferred_element_type=F32)


def scores_of(q, text, own, near, away, inside, key_factor):
    first, second = text[0].shape[0], near[0].shape[0]
    fixed = dot_t(q, jnp.concatenate([text[0], own[0]], 0)) * (LOG2E / HEAD**0.5)
    far = dot_t(q, jnp.concatenate([near[0], away[0]], 0)) * (key_factor * LOG2E)
    return jnp.concatenate([fixed[:, :first], jnp.where(inside, fixed[:, first:], far[:, :second]), far[:, second:]], 1)


def weights_of(score):
    weight = jnp.exp2(score - score.max(-1, keepdims=True))
    return weight.astype(BF16), weight.sum(-1, keepdims=True)


def mix(rounded, total, text, own, near, away, inside, value_factor):
    first, second = text[0].shape[0], near[0].shape[0]
    w_text, w_near, w_away = rounded[:, :first], rounded[:, first : first + second], rounded[:, first + second :]
    zero = jnp.zeros((), BF16)
    kept = dot(jnp.concatenate([w_text, jnp.where(inside, w_near, zero)], 1), jnp.concatenate([text[1], own[1]], 0))
    far = dot(jnp.concatenate([jnp.where(inside, zero, w_near), w_away], 1), jnp.concatenate([near[1], away[1]], 0))
    return (kept + value_factor * far) / total


def kernel_columns(ref, index):
    width = index[1]
    return ref.at[..., pl.ds(pl.multiple_of(index[0] * width, width), width)]


def run_copies(copies, sems):
    started = [pltpu.make_async_copy(a, b, sems.at[i]) for i, (a, b) in enumerate(copies)]
    for c in started:
        c.start()
    for c in started:
        c.wait()


def pack_shared_kernel(stale_ref, first_ref, *refs, layers):
    rounds = layers // 2
    layer = lax.axis_index("patch") // COLUMNS
    out_refs, sems = refs[:-1], refs[-1]
    width = out_refs[0].shape[-1]
    copies = [
        (kernel_columns(stale_ref, ((layer + k) % rounds, width)), out_refs[k]) for k in range(rounds)
    ]
    for s in range(layers):
        copies.append((kernel_columns(first_ref.at[1:], ((layer + s) % layers, width)), out_refs[rounds + s]))
    run_copies(copies, sems)


def pack_owned_kernel(first_ref, second_ref, text_first_ref, text_second_ref, *refs, layers):
    layer = lax.axis_index("patch") // COLUMNS
    out_refs, text_ref, sems = refs[:-2], refs[-2], refs[-1]
    width = text_ref.shape[-1]
    copies = []
    for s, out_ref in enumerate(out_refs):
        copies.append((kernel_columns(first_ref.at[:1], ((layer + s) % layers, width)), out_ref.at[:1]))
        copies.append((kernel_columns(second_ref, ((layer + s) % layers, width)), out_ref.at[1:]))
    for i, ref in enumerate((text_first_ref, text_second_ref)):
        copies.append((kernel_columns(ref, (layer % (layers // 2), width)), text_ref.at[2 * i : 2 * i + 2]))
    run_copies(copies, sems)


def pack(kernel, shapes, copies, *operands):
    return pl.pallas_call(
        kernel,
        out_shape=[jax.ShapeDtypeStruct(shape, BF16) for shape in shapes],
        in_specs=[pl.BlockSpec(memory_space=pl.ANY)] * len(operands),
        out_specs=[pl.BlockSpec(memory_space=pltpu.VMEM)] * len(shapes),
        scratch_shapes=[pltpu.SemaphoreType.DMA((copies,))],
        cost_estimate=pl.CostEstimate(flops=0, bytes_accessed=1 << 20, transcendentals=0),
    )(*operands)


def both_kernel(scale_ref, order_ref, queries_ref, text_ref, text_twin_ref, last_ref, last_twin_ref, *refs, parts, blocks, layers):
    sets, refs = [], list(refs)
    for p in parts:
        sets.append(refs[:p])
        refs = refs[p:]
    near_sets, away_sets = sets[:2], sets[2:]
    out_refs = refs
    rounds = layers // 2
    count, width = queries_ref.shape[1:]
    rows = count // layers
    first_row, last_row = blocks[0] * rows, (blocks[-1] + 1) * rows
    inverse = 1.0 / HEAD**0.5
    shape = (last_row - first_row, 2 * count)
    query_block = lax.broadcasted_iota(jnp.int32, shape, 0) // rows + blocks[0]
    place = lax.broadcasted_iota(jnp.int32, shape, 1)
    inside = [query_block == place // (2 * rows), query_block == place % count // rows]

    def fresh_view(pieces):
        return (pieces[1], 0) if len(pieces) == 2 else (pieces[0], layers)

    work = []
    for step in range(2):
        for head in range(width // HEAD):
            lanes = slice(head * HEAD, (head + 1) * HEAD)

            def text(i):
                at = 2 * step + i
                return jnp.where(order_ref[2, 0] == 0, text_ref[at, :, lanes], text_twin_ref[at, :, lanes])

            def fresh(pieces, i):
                ref, base = fresh_view(pieces)
                half = layers // 2
                return jnp.concatenate([ref[base + half * i + j, :, lanes] for j in range(half)], 0)

            def fresh_all(pair, i):
                return jnp.concatenate([fresh(p, i) for p in pair], 0)

            def in_patches(i):
                own, twin = (fresh(p, i) for p in near_sets)
                return jnp.concatenate([x[s * rows : (s + 1) * rows] for s in range(layers) for x in (own, twin)], 0)

            def last(i):
                return jnp.concatenate([last_ref[2 + i, :, lanes], last_twin_ref[last_twin_ref.shape[0] - 2 + i, :, lanes]], 0)

            def stale_in_patches(i):
                blocks = []
                for s in range(layers):
                    at = 2 * order_ref[1, s] + i
                    blocks.append(jnp.where(order_ref[0, s] == 0, *(p[0][at, :, lanes] for p in near_sets)))
                return jnp.concatenate(blocks, 0)

            def stale_elsewhere(i):
                return jnp.concatenate([p[0][2 * k + i, :, lanes] for p in away_sets for k in range(rounds)], 0)

            if step == 0:
                own = [in_patches(i) for i in range(2)]
                near = [stale_in_patches(i) for i in range(2)]
                away = [stale_elsewhere(i) for i in range(2)]
            else:
                own = [last(i) for i in range(2)]
                near = [fresh_all(near_sets, i) for i in range(2)]
                away = [fresh_all(away_sets, i) for i in range(2)]
            parts_of = ([text(i) for i in range(2)], own, near, away)
            work.append((step, head, lanes, parts_of))
    scores = [
        scores_of(queries_ref[step, first_row:last_row, lanes], *p, inside[step], inverse if step else scale_ref[0, head] * inverse)
        for step, head, lanes, p in work
    ]
    weights = [weights_of(s) for s in scores]
    for (step, head, lanes, p), (rounded, total) in zip(work, weights):
        result = mix(rounded, total, *p, inside[step], 1.0 if step else scale_ref[1, head])
        for i, out_ref in enumerate(out_refs):
            out_ref[step, :, lanes] = result[i * rows : (i + 1) * rows].astype(BF16)


def call_both(layers, scalars, parts, blocks, *operands):
    count, width = operands[0].shape[1:]
    rows = count // layers
    keys = 2 * operands[1].shape[1] + 8 * count
    in_vmem = pl.BlockSpec(memory_space=pltpu.VMEM)
    return pl.pallas_call(
        functools.partial(both_kernel, parts=parts, blocks=blocks, layers=layers),
        out_shape=[jax.ShapeDtypeStruct((2, rows, width), BF16)] * len(blocks),
        in_specs=[pl.BlockSpec(memory_space=pltpu.SMEM)] * len(scalars) + [in_vmem] * len(operands),
        out_specs=[in_vmem] * len(blocks),
        compiler_params=pltpu.CompilerParams(vmem_limit_bytes=32 * 1024 * 1024),
        cost_estimate=pl.CostEstimate(
            flops=4 * rows * len(blocks) * keys * width,
            bytes_accessed=4 * width * (keys + count),
            transcendentals=rows * len(blocks) * keys * width // HEAD,
        ),
    )(*scalars, *operands)


def layered_shards(layers, fresh_first, fresh_second, stale_cache, stale_exponent, text_first, text_second):
    core = lax.axis_index("uly")
    layer = lax.axis_index("patch") // COLUMNS
    rows, features = fresh_first.shape[1:]
    width = features // layers
    heads = width // HEAD
    half = features // 2
    rounds = layers // 2
    count = layers * rows
    text_rows = text_first.shape[1]

    def after(x, *needed):
        return lax.optimization_barrier((x,) + needed)[0]

    def layer_swap(x, shift):
        pairs = [(z * COLUMNS + y, (z + shift) % layers * COLUMNS + y) for z in range(layers) for y in range(COLUMNS)]
        return x if shift == 0 else lax.ppermute(x, "patch", pairs)

    def stale_round(x, k):
        pairs = []
        for z in range(layers):
            for y in range(COLUMNS):
                for u in range(2):
                    to = (u * rounds + (z + k) % rounds) * COLUMNS + y
                    pairs.append(((z * COLUMNS + y) * 2 + u, to * 2 + z // rounds))
        return lax.ppermute(x, ("patch", "uly"), pairs)

    def other_column(x):
        return lax.ppermute(x, "patch", [(p, p ^ 1) for p in range(layers * COLUMNS)])

    def other_core(x):
        return lax.ppermute(x, "uly", [(0, 1), (1, 0)])

    def columns_of(x, index):
        return lax.dynamic_slice_in_dim(x, index * width, width, x.ndim - 1)

    shared = [columns_of(stale_cache, (layer + k) % rounds) for k in range(rounds)]
    shared += [columns_of(fresh_first[1:], (layer + s) % layers) for s in range(layers)]
    *owned, text = pack(
        functools.partial(pack_owned_kernel, layers=layers),
        [(4, rows, width)] * layers + [(4, text_rows, width)],
        2 * layers + 2,
        after(fresh_first, shared),
        fresh_second,
        text_first,
        text_second,
    )
    stale = [stale_round(shared[k], k) for k in range(rounds)]
    fresh = [layer_swap(shared[rounds + s], s) for s in range(layers)]
    fresh[0] = after(fresh[0], owned)
    fresh_block = jnp.concatenate(fresh, 1).reshape(layers, 2 * rows, width)
    stale_block = jnp.concatenate(stale, 0)
    near = jnp.concatenate([stale_block, fresh_block], 0)
    away = [other_column(near)]
    owned = [owned[0], owned[1], after(owned[2], near), after(owned[3], near)]
    owned = {s: layer_swap(owned[s], s) for s in (0, 2, 1, 3)}
    owned = [owned[s] for s in range(layers)]
    away_twin = [other_core(away[0][:layers]), other_core(away[0][layers:])]
    last = jnp.concatenate(owned, 1)
    near_twin = [other_core(near)]
    last_twin = other_core(last)
    text_twin = other_core(after(text, owned[1]))
    sets = [[near], near_twin, away, away_twin]

    scales = jnp.exp2(lax.dynamic_slice_in_dim(stale_exponent, layer * heads, heads, 1).astype(F32))
    source = [(layer - s) % layers for s in range(layers)]
    order = jnp.stack(
        [jnp.stack([(L // rounds != core).astype(jnp.int32) for L in source]), jnp.stack([(L - layer) % rounds for L in source]), jnp.full((layers,), (layer // rounds != core).astype(jnp.int32))]
    )
    parts = tuple(len(p) for p in sets)
    flat = [p for pieces in sets for p in pieces]
    operands = [last[:2], text, text_twin, last, last_twin, *flat]
    sent = call_both(layers, [scales, order], parts, tuple(range(1, layers)), *operands)
    (kept,) = call_both(layers, [scales, order], parts, (0,), *operands)
    blocks = [kept, *sent]

    out = jnp.zeros((2, rows, features), BF16)
    for s in range(layers):
        out = lax.dynamic_update_slice_in_dim(out, layer_swap(blocks[s], -s), (layer + s) % layers * width, 2)
    return out[0], out[1]


def solution(mesh):
    placed = (
        P(None, ("group", "patch", "uly"), None),
        P(None, ("group", "patch", "uly"), None),
        P(None, ("group", "patch"), "uly"),
        P("group", None),
        P(None, "group", "uly"),
        P(None, "group", "uly"),
    )

    def shards(*arrays):
        layers = mesh.shape["patch"] // COLUMNS
        heads = arrays[0].shape[2] // HEAD
        if mesh.shape["uly"] == 2 and layers == 4 and heads % layers == 0:
            return layered_shards(layers, *arrays)
        return general_shards(*arrays)

    return jax.shard_map(
        shards,
        mesh=mesh,
        in_specs=placed,
        out_specs=(P(("group", "patch", "uly"), None), P(("group", "patch", "uly"), None)),
        check_vma=False,
    )
```

```python
import functools

import jax
import jax.numpy as jnp
from jax import lax
from jax.experimental import pallas as pl
from jax.experimental.pallas import tpu as pltpu
from jax.sharding import PartitionSpec as P

HEAD = 128
LOG2E = 1.4426950408889634
COLUMNS = 2
BF16 = jnp.bfloat16
F32 = jnp.float32


def heads_view(array):
    return array.reshape(array.shape[0], array.shape[1] // HEAD, HEAD)


def absorb(carry, queries, keys_rows, values, key_scale, value_scale, keep):
    top, total, accum = carry
    inverse = 1.0 / HEAD**0.5
    score = jnp.einsum("qhd,khd->hqk", queries, keys_rows, preferred_element_type=F32)
    score = score * (key_scale * inverse)[:, None, None]
    if keep is not None:
        score = jnp.where(keep[None, None, :], score, -jnp.inf)
    new_top = jnp.maximum(top, score.max(-1))
    fade = jnp.exp(top - new_top)
    weight = jnp.exp(score - new_top[:, :, None])
    total = total * fade + weight.sum(-1)
    addend = jnp.einsum("hqk,khd->qhd", weight.astype(BF16), values, preferred_element_type=F32)
    accum = accum * fade.T[:, :, None] + addend * value_scale[None, :, None]
    return (new_top, total, accum)


def general_step(mine, text, far, keep, key_scale, value_scale):
    queries = heads_view(mine[0])
    rows, local_heads = queries.shape[:2]
    unit = jnp.ones((local_heads,), F32)
    carry = (
        jnp.full((local_heads, rows), -jnp.inf, F32),
        jnp.zeros((local_heads, rows), F32),
        jnp.zeros((rows, local_heads, HEAD), F32),
    )
    carry = absorb(carry, queries, heads_view(text[0]), heads_view(text[1]), unit, unit, None)
    carry = absorb(carry, queries, heads_view(mine[1]), heads_view(mine[2]), unit, unit, None)
    carry = absorb(carry, queries, heads_view(far[0]), heads_view(far[1]), key_scale, value_scale, keep)
    top, total, accum = carry
    result = (accum / total.T[:, :, None]).reshape(rows, local_heads * HEAD).astype(BF16)
    return lax.all_to_all(result, "uly", split_axis=0, concat_axis=1, tiled=True)


def general_shards(fresh_first, fresh_second, stale_cache, stale_exponent, text_first, text_second):
    local_heads = stale_exponent.shape[1] // lax.axis_size("uly")
    first_head = lax.axis_index("uly") * local_heads
    exponents = lax.dynamic_slice_in_dim(stale_exponent, first_head, local_heads, 1)
    scales = jnp.exp2(exponents.astype(F32))
    unit = jnp.ones((local_heads,), F32)
    mine_first = lax.all_to_all(fresh_first, "uly", split_axis=2, concat_axis=1, tiled=True)
    mine_second = lax.all_to_all(fresh_second, "uly", split_axis=2, concat_axis=1, tiled=True)
    rows = mine_first.shape[1]
    own_start = lax.axis_index("patch") * rows
    stale = lax.all_gather(stale_cache, "patch", axis=1, tiled=True)
    refreshed = lax.all_gather(mine_first[1:], "patch", axis=1, tiled=True)
    places = jnp.arange(stale.shape[1], dtype=jnp.int32)
    keep = (places < own_start) | (places >= own_start + rows)
    return (
        general_step(mine_first, text_first, stale, keep, scales[0], scales[1]),
        general_step(mine_second, text_second, refreshed, keep, unit, unit),
    )


def dot_t(a, b):
    return lax.dot_general(a, b, (((1,), (1,)), ((), ())), preferred_element_type=F32)


def dot(a, b):
    return jnp.dot(a, b, preferred_element_type=F32)


def scores_of(q, text, own, near, away, inside, key_factor):
    first, second = text[0].shape[0], near[0].shape[0]
    fixed = dot_t(q, jnp.concatenate([text[0], own[0]], 0)) * (LOG2E / HEAD**0.5)
    far = dot_t(q, jnp.concatenate([near[0], away[0]], 0)) * (key_factor * LOG2E)
    return jnp.concatenate([fixed[:, :first], jnp.where(inside, fixed[:, first:], far[:, :second]), far[:, second:]], 1)


def weights_of(score):
    weight = jnp.exp2(score - score.max(-1, keepdims=True))
    return weight.astype(BF16), weight.sum(-1, keepdims=True)


def mix(rounded, total, text, own, near, away, inside, value_factor):
    first, second = text[0].shape[0], near[0].shape[0]
    w_text, w_near, w_away = rounded[:, :first], rounded[:, first : first + second], rounded[:, first + second :]
    zero = jnp.zeros((), BF16)
    kept = dot(jnp.concatenate([w_text, jnp.where(inside, w_near, zero)], 1), jnp.concatenate([text[1], own[1]], 0))
    far = dot(jnp.concatenate([jnp.where(inside, zero, w_near), w_away], 1), jnp.concatenate([near[1], away[1]], 0))
    return (kept + value_factor * far) / total


def kernel_columns(ref, index):
    width = index[1]
    return ref.at[..., pl.ds(pl.multiple_of(index[0] * width, width), width)]


def run_copies(copies, sems):
    started = [pltpu.make_async_copy(a, b, sems.at[i]) for i, (a, b) in enumerate(copies)]
    for c in started:
        c.start()
    for c in started:
        c.wait()


def pack_shared_kernel(stale_ref, first_ref, *refs, layers):
    rounds = layers // 2
    layer = lax.axis_index("patch") // COLUMNS
    out_refs, sems = refs[:-1], refs[-1]
    width = out_refs[0].shape[-1]
    copies = [
        (kernel_columns(stale_ref, ((layer + k) % rounds, width)), out_refs[k]) for k in range(rounds)
    ]
    for s in range(layers):
        copies.append((kernel_columns(first_ref.at[1:], ((layer + s) % layers, width)), out_refs[rounds + s]))
    run_copies(copies, sems)


def pack_owned_kernel(first_ref, second_ref, text_first_ref, text_second_ref, *refs, layers):
    layer = lax.axis_index("patch") // COLUMNS
    out_refs, text_ref, sems = refs[:-2], refs[-2], refs[-1]
    width = text_ref.shape[-1]
    copies = []
    for s, out_ref in enumerate(out_refs):
        copies.append((kernel_columns(first_ref.at[:1], ((layer + s) % layers, width)), out_ref.at[:1]))
        copies.append((kernel_columns(second_ref, ((layer + s) % layers, width)), out_ref.at[1:]))
    for i, ref in enumerate((text_first_ref, text_second_ref)):
        copies.append((kernel_columns(ref, (layer % (layers // 2), width)), text_ref.at[2 * i : 2 * i + 2]))
    run_copies(copies, sems)


def pack(kernel, shapes, copies, *operands):
    return pl.pallas_call(
        kernel,
        out_shape=[jax.ShapeDtypeStruct(shape, BF16) for shape in shapes],
        in_specs=[pl.BlockSpec(memory_space=pl.ANY)] * len(operands),
        out_specs=[pl.BlockSpec(memory_space=pltpu.VMEM)] * len(shapes),
        scratch_shapes=[pltpu.SemaphoreType.DMA((copies,))],
        cost_estimate=pl.CostEstimate(flops=0, bytes_accessed=1 << 20, transcendentals=0),
    )(*operands)


def both_kernel(scale_ref, order_ref, queries_ref, text_ref, text_twin_ref, last_ref, last_twin_ref, *refs, parts, blocks, layers):
    sets, refs = [], list(refs)
    for p in parts:
        sets.append(refs[:p])
        refs = refs[p:]
    near_sets, away_sets = sets[:2], sets[2:]
    out_refs = refs
    rounds = layers // 2
    count, width = queries_ref.shape[1:]
    rows = count // layers
    first_row, last_row = blocks[0] * rows, (blocks[-1] + 1) * rows
    inverse = 1.0 / HEAD**0.5
    shape = (last_row - first_row, 2 * count)
    query_block = lax.broadcasted_iota(jnp.int32, shape, 0) // rows + blocks[0]
    place = lax.broadcasted_iota(jnp.int32, shape, 1)
    inside = [query_block == place // (2 * rows), query_block == place % count // rows]

    def fresh_view(pieces):
        return (pieces[1], 0) if len(pieces) == 2 else (pieces[0], layers)

    work = []
    for step in range(2):
        for head in range(width // HEAD):
            lanes = slice(head * HEAD, (head + 1) * HEAD)

            def text(i):
                at = 2 * step + i
                return jnp.where(order_ref[2, 0] == 0, text_ref[at, :, lanes], text_twin_ref[at, :, lanes])

            def fresh(pieces, i):
                ref, base = fresh_view(pieces)
                half = layers // 2
                return jnp.concatenate([ref[base + half * i + j, :, lanes] for j in range(half)], 0)

            def fresh_all(pair, i):
                return jnp.concatenate([fresh(p, i) for p in pair], 0)

            def in_patches(i):
                own, twin = (fresh(p, i) for p in near_sets)
                return jnp.concatenate([x[s * rows : (s + 1) * rows] for s in range(layers) for x in (own, twin)], 0)

            def last(i):
                return jnp.concatenate([last_ref[2 + i, :, lanes], last_twin_ref[last_twin_ref.shape[0] - 2 + i, :, lanes]], 0)

            def stale_in_patches(i):
                blocks = []
                for s in range(layers):
                    at = 2 * order_ref[1, s] + i
                    blocks.append(jnp.where(order_ref[0, s] == 0, *(p[0][at, :, lanes] for p in near_sets)))
                return jnp.concatenate(blocks, 0)

            def stale_elsewhere(i):
                return jnp.concatenate([p[0][2 * k + i, :, lanes] for p in away_sets for k in range(rounds)], 0)

            if step == 0:
                own = [in_patches(i) for i in range(2)]
                near = [stale_in_patches(i) for i in range(2)]
                away = [stale_elsewhere(i) for i in range(2)]
            else:
                own = [last(i) for i in range(2)]
                near = [fresh_all(near_sets, i) for i in range(2)]
                away = [fresh_all(away_sets, i) for i in range(2)]
            parts_of = ([text(i) for i in range(2)], own, near, away)
            work.append((step, head, lanes, parts_of))
    scores = [
        scores_of(queries_ref[step, first_row:last_row, lanes], *p, inside[step], inverse if step else scale_ref[0, head] * inverse)
        for step, head, lanes, p in work
    ]
    weights = [weights_of(s) for s in scores]
    for (step, head, lanes, p), (rounded, total) in zip(work, weights):
        result = mix(rounded, total, *p, inside[step], 1.0 if step else scale_ref[1, head])
        for i, out_ref in enumerate(out_refs):
            out_ref[step, :, lanes] = result[i * rows : (i + 1) * rows].astype(BF16)


def call_both(layers, scalars, parts, blocks, *operands):
    count, width = operands[0].shape[1:]
    rows = count // layers
    keys = 2 * operands[1].shape[1] + 8 * count
    in_vmem = pl.BlockSpec(memory_space=pltpu.VMEM)
    return pl.pallas_call(
        functools.partial(both_kernel, parts=parts, blocks=blocks, layers=layers),
        out_shape=[jax.ShapeDtypeStruct((2, rows, width), BF16)] * len(blocks),
        in_specs=[pl.BlockSpec(memory_space=pltpu.SMEM)] * len(scalars) + [in_vmem] * len(operands),
        out_specs=[in_vmem] * len(blocks),
        compiler_params=pltpu.CompilerParams(vmem_limit_bytes=32 * 1024 * 1024),
        cost_estimate=pl.CostEstimate(
            flops=4 * rows * len(blocks) * keys * width,
            bytes_accessed=4 * width * (keys + count),
            transcendentals=rows * len(blocks) * keys * width // HEAD,
        ),
    )(*scalars, *operands)


def layered_shards(layers, fresh_first, fresh_second, stale_cache, stale_exponent, text_first, text_second):
    core = lax.axis_index("uly")
    layer = lax.axis_index("patch") // COLUMNS
    rows, features = fresh_first.shape[1:]
    width = features // layers
    heads = width // HEAD
    half = features // 2
    rounds = layers // 2
    count = layers * rows
    text_rows = text_first.shape[1]

    def after(x, *needed):
        return lax.optimization_barrier((x,) + needed)[0]

    def layer_swap(x, shift):
        pairs = [(z * COLUMNS + y, (z + shift) % layers * COLUMNS + y) for z in range(layers) for y in range(COLUMNS)]
        return x if shift == 0 else lax.ppermute(x, "patch", pairs)

    def stale_round(x, k):
        pairs = []
        for z in range(layers):
            for y in range(COLUMNS):
                for u in range(2):
                    to = (u * rounds + (z + k) % rounds) * COLUMNS + y
                    pairs.append(((z * COLUMNS + y) * 2 + u, to * 2 + z // rounds))
        return lax.ppermute(x, ("patch", "uly"), pairs)

    def other_column(x):
        return lax.ppermute(x, "patch", [(p, p ^ 1) for p in range(layers * COLUMNS)])

    def other_core(x):
        return lax.ppermute(x, "uly", [(0, 1), (1, 0)])

    def columns_of(x, index):
        return lax.dynamic_slice_in_dim(x, index * width, width, x.ndim - 1)

    shared = [columns_of(stale_cache, (layer + k) % rounds) for k in range(rounds)]
    shared += [columns_of(fresh_first[1:], (layer + s) % layers) for s in range(layers)]
    *owned, text = pack(
        functools.partial(pack_owned_kernel, layers=layers),
        [(4, rows, width)] * layers + [(4, text_rows, width)],
        2 * layers + 2,
        after(fresh_first, shared),
        fresh_second,
        text_first,
        text_second,
    )
    stale = [stale_round(shared[k], k) for k in range(rounds)]
    fresh = [layer_swap(shared[rounds + s], s) for s in range(layers)]
    fresh[0] = after(fresh[0], owned)
    fresh_block = jnp.concatenate(fresh, 1).reshape(layers, 2 * rows, width)
    stale_block = jnp.concatenate(stale, 0)
    near = jnp.concatenate([stale_block, fresh_block], 0)
    away = [other_column(near)]
    owned = [owned[0], owned[1], after(owned[2], near), after(owned[3], near)]
    owned = {s: layer_swap(owned[s], s) for s in (0, 3, 2, 1)}
    owned = [owned[s] for s in range(layers)]
    away_twin = [other_core(away[0][:layers]), other_core(away[0][layers:])]
    last = jnp.concatenate(owned, 1)
    near_twin = [other_core(near)]
    last_twin = other_core(last)
    text_twin = other_core(after(text, owned[1]))
    sets = [[near], near_twin, away, away_twin]

    scales = jnp.exp2(lax.dynamic_slice_in_dim(stale_exponent, layer * heads, heads, 1).astype(F32))
    source = [(layer - s) % layers for s in range(layers)]
    order = jnp.stack(
        [jnp.stack([(L // rounds != core).astype(jnp.int32) for L in source]), jnp.stack([(L - layer) % rounds for L in source]), jnp.full((layers,), (layer // rounds != core).astype(jnp.int32))]
    )
    parts = tuple(len(p) for p in sets)
    flat = [p for pieces in sets for p in pieces]
    operands = [last[:2], text, text_twin, last, last_twin, *flat]
    sent = call_both(layers, [scales, order], parts, tuple(range(1, layers)), *operands)
    (kept,) = call_both(layers, [scales, order], parts, (0,), *operands)
    blocks = [kept, *sent]

    out = jnp.zeros((2, rows, features), BF16)
    for s in (0, 2, 3, 1):
        out = lax.dynamic_update_slice_in_dim(out, layer_swap(blocks[s], -s), (layer + s) % layers * width, 2)
    return out[0], out[1]


def solution(mesh):
    placed = (
        P(None, ("group", "patch", "uly"), None),
        P(None, ("group", "patch", "uly"), None),
        P(None, ("group", "patch"), "uly"),
        P("group", None),
        P(None, "group", "uly"),
        P(None, "group", "uly"),
    )

    def shards(*arrays):
        layers = mesh.shape["patch"] // COLUMNS
        heads = arrays[0].shape[2] // HEAD
        if mesh.shape["uly"] == 2 and layers == 4 and heads % layers == 0:
            return layered_shards(layers, *arrays)
        return general_shards(*arrays)

    return jax.shard_map(
        shards,
        mesh=mesh,
        in_specs=placed,
        out_specs=(P(("group", "patch", "uly"), None), P(("group", "patch", "uly"), None)),
        check_vma=False,
    )
```

```python
import functools

import jax
import jax.numpy as jnp
from jax import lax
from jax.experimental import pallas as pl
from jax.experimental.pallas import tpu as pltpu
from jax.sharding import PartitionSpec as P

HEAD = 128
LOG2E = 1.4426950408889634
COLUMNS = 2
BF16 = jnp.bfloat16
F32 = jnp.float32


def heads_view(array):
    return array.reshape(array.shape[0], array.shape[1] // HEAD, HEAD)


def absorb(carry, queries, keys_rows, values, key_scale, value_scale, keep):
    top, total, accum = carry
    inverse = 1.0 / HEAD**0.5
    score = jnp.einsum("qhd,khd->hqk", queries, keys_rows, preferred_element_type=F32)
    score = score * (key_scale * inverse)[:, None, None]
    if keep is not None:
        score = jnp.where(keep[None, None, :], score, -jnp.inf)
    new_top = jnp.maximum(top, score.max(-1))
    fade = jnp.exp(top - new_top)
    weight = jnp.exp(score - new_top[:, :, None])
    total = total * fade + weight.sum(-1)
    addend = jnp.einsum("hqk,khd->qhd", weight.astype(BF16), values, preferred_element_type=F32)
    accum = accum * fade.T[:, :, None] + addend * value_scale[None, :, None]
    return (new_top, total, accum)


def general_step(mine, text, far, keep, key_scale, value_scale):
    queries = heads_view(mine[0])
    rows, local_heads = queries.shape[:2]
    unit = jnp.ones((local_heads,), F32)
    carry = (
        jnp.full((local_heads, rows), -jnp.inf, F32),
        jnp.zeros((local_heads, rows), F32),
        jnp.zeros((rows, local_heads, HEAD), F32),
    )
    carry = absorb(carry, queries, heads_view(text[0]), heads_view(text[1]), unit, unit, None)
    carry = absorb(carry, queries, heads_view(mine[1]), heads_view(mine[2]), unit, unit, None)
    carry = absorb(carry, queries, heads_view(far[0]), heads_view(far[1]), key_scale, value_scale, keep)
    top, total, accum = carry
    result = (accum / total.T[:, :, None]).reshape(rows, local_heads * HEAD).astype(BF16)
    return lax.all_to_all(result, "uly", split_axis=0, concat_axis=1, tiled=True)


def general_shards(fresh_first, fresh_second, stale_cache, stale_exponent, text_first, text_second):
    local_heads = stale_exponent.shape[1] // lax.axis_size("uly")
    first_head = lax.axis_index("uly") * local_heads
    exponents = lax.dynamic_slice_in_dim(stale_exponent, first_head, local_heads, 1)
    scales = jnp.exp2(exponents.astype(F32))
    unit = jnp.ones((local_heads,), F32)
    mine_first = lax.all_to_all(fresh_first, "uly", split_axis=2, concat_axis=1, tiled=True)
    mine_second = lax.all_to_all(fresh_second, "uly", split_axis=2, concat_axis=1, tiled=True)
    rows = mine_first.shape[1]
    own_start = lax.axis_index("patch") * rows
    stale = lax.all_gather(stale_cache, "patch", axis=1, tiled=True)
    refreshed = lax.all_gather(mine_first[1:], "patch", axis=1, tiled=True)
    places = jnp.arange(stale.shape[1], dtype=jnp.int32)
    keep = (places < own_start) | (places >= own_start + rows)
    return (
        general_step(mine_first, text_first, stale, keep, scales[0], scales[1]),
        general_step(mine_second, text_second, refreshed, keep, unit, unit),
    )


def dot_t(a, b):
    return lax.dot_general(a, b, (((1,), (1,)), ((), ())), preferred_element_type=F32)


def dot(a, b):
    return jnp.dot(a, b, preferred_element_type=F32)


def scores_of(q, text, own, near, away, inside, key_factor):
    first, second = text[0].shape[0], near[0].shape[0]
    fixed = dot_t(q, jnp.concatenate([text[0], own[0]], 0)) * (LOG2E / HEAD**0.5)
    far = dot_t(q, jnp.concatenate([near[0], away[0]], 0)) * (key_factor * LOG2E)
    return jnp.concatenate([fixed[:, :first], jnp.where(inside, fixed[:, first:], far[:, :second]), far[:, second:]], 1)


def weights_of(score):
    weight = jnp.exp2(score - score.max(-1, keepdims=True))
    return weight.astype(BF16), weight.sum(-1, keepdims=True)


def mix(rounded, total, text, own, near, away, inside, value_factor):
    first, second = text[0].shape[0], near[0].shape[0]
    w_text, w_near, w_away = rounded[:, :first], rounded[:, first : first + second], rounded[:, first + second :]
    zero = jnp.zeros((), BF16)
    kept = dot(jnp.concatenate([w_text, jnp.where(inside, w_near, zero)], 1), jnp.concatenate([text[1], own[1]], 0))
    far = dot(jnp.concatenate([jnp.where(inside, zero, w_near), w_away], 1), jnp.concatenate([near[1], away[1]], 0))
    return (kept + value_factor * far) / total


def kernel_columns(ref, index):
    width = index[1]
    return ref.at[..., pl.ds(pl.multiple_of(index[0] * width, width), width)]


def run_copies(copies, sems):
    started = [pltpu.make_async_copy(a, b, sems.at[i]) for i, (a, b) in enumerate(copies)]
    for c in started:
        c.start()
    for c in started:
        c.wait()


def pack_shared_kernel(stale_ref, first_ref, *refs, layers):
    rounds = layers // 2
    layer = lax.axis_index("patch") // COLUMNS
    out_refs, sems = refs[:-1], refs[-1]
    width = out_refs[0].shape[-1]
    copies = [
        (kernel_columns(stale_ref, ((layer + k) % rounds, width)), out_refs[k]) for k in range(rounds)
    ]
    for s in range(layers):
        copies.append((kernel_columns(first_ref.at[1:], ((layer + s) % layers, width)), out_refs[rounds + s]))
    run_copies(copies, sems)


def pack_owned_kernel(first_ref, second_ref, text_first_ref, text_second_ref, *refs, layers):
    layer = lax.axis_index("patch") // COLUMNS
    out_refs, text_ref, sems = refs[:-2], refs[-2], refs[-1]
    width = text_ref.shape[-1]
    copies = []
    for s, out_ref in enumerate(out_refs):
        copies.append((kernel_columns(first_ref.at[:1], ((layer + s) % layers, width)), out_ref.at[:1]))
        copies.append((kernel_columns(second_ref, ((layer + s) % layers, width)), out_ref.at[1:]))
    for i, ref in enumerate((text_first_ref, text_second_ref)):
        copies.append((kernel_columns(ref, (layer % (layers // 2), width)), text_ref.at[2 * i : 2 * i + 2]))
    run_copies(copies, sems)


def pack(kernel, shapes, copies, *operands):
    return pl.pallas_call(
        kernel,
        out_shape=[jax.ShapeDtypeStruct(shape, BF16) for shape in shapes],
        in_specs=[pl.BlockSpec(memory_space=pl.ANY)] * len(operands),
        out_specs=[pl.BlockSpec(memory_space=pltpu.VMEM)] * len(shapes),
        scratch_shapes=[pltpu.SemaphoreType.DMA((copies,))],
        cost_estimate=pl.CostEstimate(flops=0, bytes_accessed=1 << 20, transcendentals=0),
    )(*operands)


def both_kernel(scale_ref, order_ref, queries_ref, text_ref, text_twin_ref, last_ref, last_twin_ref, *refs, parts, blocks, layers):
    sets, refs = [], list(refs)
    for p in parts:
        sets.append(refs[:p])
        refs = refs[p:]
    near_sets, away_sets = sets[:2], sets[2:]
    out_refs = refs
    rounds = layers // 2
    count, width = queries_ref.shape[1:]
    rows = count // layers
    first_row, last_row = blocks[0] * rows, (blocks[-1] + 1) * rows
    inverse = 1.0 / HEAD**0.5
    shape = (last_row - first_row, 2 * count)
    query_block = lax.broadcasted_iota(jnp.int32, shape, 0) // rows + blocks[0]
    place = lax.broadcasted_iota(jnp.int32, shape, 1)
    inside = [query_block == place // (2 * rows), query_block == place % count // rows]

    def fresh_view(pieces):
        return (pieces[1], 0) if len(pieces) == 2 else (pieces[0], layers)

    work = []
    for step in range(2):
        for head in range(width // HEAD):
            lanes = slice(head * HEAD, (head + 1) * HEAD)

            def text(i):
                at = 2 * step + i
                return jnp.where(order_ref[2, 0] == 0, text_ref[at, :, lanes], text_twin_ref[at, :, lanes])

            def fresh(pieces, i):
                ref, base = fresh_view(pieces)
                half = layers // 2
                return jnp.concatenate([ref[base + half * i + j, :, lanes] for j in range(half)], 0)

            def fresh_all(pair, i):
                return jnp.concatenate([fresh(p, i) for p in pair], 0)

            def in_patches(i):
                own, twin = (fresh(p, i) for p in near_sets)
                return jnp.concatenate([x[s * rows : (s + 1) * rows] for s in range(layers) for x in (own, twin)], 0)

            def last(i):
                return jnp.concatenate([last_ref[2 + i, :, lanes], last_twin_ref[last_twin_ref.shape[0] - 2 + i, :, lanes]], 0)

            def stale_in_patches(i):
                blocks = []
                for s in range(layers):
                    at = 2 * order_ref[1, s] + i
                    blocks.append(jnp.where(order_ref[0, s] == 0, *(p[0][at, :, lanes] for p in near_sets)))
                return jnp.concatenate(blocks, 0)

            def stale_elsewhere(i):
                return jnp.concatenate([p[0][2 * k + i, :, lanes] for p in away_sets for k in range(rounds)], 0)

            if step == 0:
                own = [in_patches(i) for i in range(2)]
                near = [stale_in_patches(i) for i in range(2)]
                away = [stale_elsewhere(i) for i in range(2)]
            else:
                own = [last(i) for i in range(2)]
                near = [fresh_all(near_sets, i) for i in range(2)]
                away = [fresh_all(away_sets, i) for i in range(2)]
            parts_of = ([text(i) for i in range(2)], own, near, away)
            work.append((step, head, lanes, parts_of))
    scores = [
        scores_of(queries_ref[step, first_row:last_row, lanes], *p, inside[step], inverse if step else scale_ref[0, head] * inverse)
        for step, head, lanes, p in work
    ]
    weights = [weights_of(s) for s in scores]
    for (step, head, lanes, p), (rounded, total) in zip(work, weights):
        result = mix(rounded, total, *p, inside[step], 1.0 if step else scale_ref[1, head])
        for i, out_ref in enumerate(out_refs):
            out_ref[step, :, lanes] = result[i * rows : (i + 1) * rows].astype(BF16)


def call_both(layers, scalars, parts, blocks, *operands):
    count, width = operands[0].shape[1:]
    rows = count // layers
    keys = 2 * operands[1].shape[1] + 8 * count
    in_vmem = pl.BlockSpec(memory_space=pltpu.VMEM)
    return pl.pallas_call(
        functools.partial(both_kernel, parts=parts, blocks=blocks, layers=layers),
        out_shape=[jax.ShapeDtypeStruct((2, rows, width), BF16)] * len(blocks),
        in_specs=[pl.BlockSpec(memory_space=pltpu.SMEM)] * len(scalars) + [in_vmem] * len(operands),
        out_specs=[in_vmem] * len(blocks),
        compiler_params=pltpu.CompilerParams(vmem_limit_bytes=32 * 1024 * 1024),
        cost_estimate=pl.CostEstimate(
            flops=4 * rows * len(blocks) * keys * width,
            bytes_accessed=4 * width * (keys + count),
            transcendentals=rows * len(blocks) * keys * width // HEAD,
        ),
    )(*scalars, *operands)


def layered_shards(layers, fresh_first, fresh_second, stale_cache, stale_exponent, text_first, text_second):
    core = lax.axis_index("uly")
    layer = lax.axis_index("patch") // COLUMNS
    rows, features = fresh_first.shape[1:]
    width = features // layers
    heads = width // HEAD
    half = features // 2
    rounds = layers // 2
    count = layers * rows
    text_rows = text_first.shape[1]

    def after(x, *needed):
        return lax.optimization_barrier((x,) + needed)[0]

    def layer_swap(x, shift):
        pairs = [(z * COLUMNS + y, (z + shift) % layers * COLUMNS + y) for z in range(layers) for y in range(COLUMNS)]
        return x if shift == 0 else lax.ppermute(x, "patch", pairs)

    def stale_round(x, k):
        pairs = []
        for z in range(layers):
            for y in range(COLUMNS):
                for u in range(2):
                    to = (u * rounds + (z + k) % rounds) * COLUMNS + y
                    pairs.append(((z * COLUMNS + y) * 2 + u, to * 2 + z // rounds))
        return lax.ppermute(x, ("patch", "uly"), pairs)

    def other_column(x):
        return lax.ppermute(x, "patch", [(p, p ^ 1) for p in range(layers * COLUMNS)])

    def other_core(x):
        return lax.ppermute(x, "uly", [(0, 1), (1, 0)])

    def columns_of(x, index):
        return lax.dynamic_slice_in_dim(x, index * width, width, x.ndim - 1)

    shared = [columns_of(stale_cache, (layer + k) % rounds) for k in range(rounds)]
    away_parts = [columns_of(fresh_first[1:], (layer + s) % layers) for s in range(1, layers)]
    shared += [columns_of(after(fresh_first, *away_parts)[1:], layer), *away_parts]
    *owned, text = pack(
        functools.partial(pack_owned_kernel, layers=layers),
        [(4, rows, width)] * layers + [(4, text_rows, width)],
        2 * layers + 2,
        after(fresh_first, shared),
        fresh_second,
        text_first,
        text_second,
    )
    stale = [stale_round(shared[k], k) for k in range(rounds)]
    fresh = [layer_swap(shared[rounds + s], s) for s in range(layers)]
    fresh[0] = after(fresh[0], owned)
    fresh_block = jnp.concatenate(fresh, 1).reshape(layers, 2 * rows, width)
    stale_block = jnp.concatenate(stale, 0)
    near = jnp.concatenate([stale_block, fresh_block], 0)
    away = [other_column(near)]
    owned = [owned[0], owned[1], after(owned[2], near), after(owned[3], near)]
    owned = {s: layer_swap(owned[s], s) for s in (0, 3, 2, 1)}
    owned = [owned[s] for s in range(layers)]
    away_twin = [other_core(away[0][:layers]), other_core(away[0][layers:])]
    last = jnp.concatenate(owned, 1)
    near_twin = [other_core(near)]
    last_twin = other_core(last)
    text_twin = other_core(after(text, owned[1]))
    sets = [[near], near_twin, away, away_twin]

    scales = jnp.exp2(lax.dynamic_slice_in_dim(stale_exponent, layer * heads, heads, 1).astype(F32))
    source = [(layer - s) % layers for s in range(layers)]
    order = jnp.stack(
        [jnp.stack([(L // rounds != core).astype(jnp.int32) for L in source]), jnp.stack([(L - layer) % rounds for L in source]), jnp.full((layers,), (layer // rounds != core).astype(jnp.int32))]
    )
    parts = tuple(len(p) for p in sets)
    flat = [p for pieces in sets for p in pieces]
    operands = [last[:2], text, text_twin, last, last_twin, *flat]
    sent = call_both(layers, [scales, order], parts, tuple(range(1, layers)), *operands)
    (kept,) = call_both(layers, [scales, order], parts, (0,), *operands)
    blocks = [kept, *sent]

    out = jnp.zeros((2, rows, features), BF16)
    for s in (0, 2, 3, 1):
        out = lax.dynamic_update_slice_in_dim(out, layer_swap(blocks[s], -s), (layer + s) % layers * width, 2)
    return out[0], out[1]


def solution(mesh):
    placed = (
        P(None, ("group", "patch", "uly"), None),
        P(None, ("group", "patch", "uly"), None),
        P(None, ("group", "patch"), "uly"),
        P("group", None),
        P(None, "group", "uly"),
        P(None, "group", "uly"),
    )

    def shards(*arrays):
        layers = mesh.shape["patch"] // COLUMNS
        heads = arrays[0].shape[2] // HEAD
        if mesh.shape["uly"] == 2 and layers == 4 and heads % layers == 0:
            return layered_shards(layers, *arrays)
        return general_shards(*arrays)

    return jax.shard_map(
        shards,
        mesh=mesh,
        in_specs=placed,
        out_specs=(P(("group", "patch", "uly"), None), P(("group", "patch", "uly"), None)),
        check_vma=False,
    )
```

```python
import functools

import jax
import jax.numpy as jnp
from jax import lax
from jax.experimental import pallas as pl
from jax.experimental.pallas import tpu as pltpu
from jax.sharding import PartitionSpec as P

HEAD = 128
LOG2E = 1.4426950408889634
COLUMNS = 2
BF16 = jnp.bfloat16
F32 = jnp.float32


def heads_view(array):
    return array.reshape(array.shape[0], array.shape[1] // HEAD, HEAD)


def absorb(carry, queries, keys_rows, values, key_scale, value_scale, keep):
    top, total, accum = carry
    inverse = 1.0 / HEAD**0.5
    score = jnp.einsum("qhd,khd->hqk", queries, keys_rows, preferred_element_type=F32)
    score = score * (key_scale * inverse)[:, None, None]
    if keep is not None:
        score = jnp.where(keep[None, None, :], score, -jnp.inf)
    new_top = jnp.maximum(top, score.max(-1))
    fade = jnp.exp(top - new_top)
    weight = jnp.exp(score - new_top[:, :, None])
    total = total * fade + weight.sum(-1)
    addend = jnp.einsum("hqk,khd->qhd", weight.astype(BF16), values, preferred_element_type=F32)
    accum = accum * fade.T[:, :, None] + addend * value_scale[None, :, None]
    return (new_top, total, accum)


def general_step(mine, text, far, keep, key_scale, value_scale):
    queries = heads_view(mine[0])
    rows, local_heads = queries.shape[:2]
    unit = jnp.ones((local_heads,), F32)
    carry = (
        jnp.full((local_heads, rows), -jnp.inf, F32),
        jnp.zeros((local_heads, rows), F32),
        jnp.zeros((rows, local_heads, HEAD), F32),
    )
    carry = absorb(carry, queries, heads_view(text[0]), heads_view(text[1]), unit, unit, None)
    carry = absorb(carry, queries, heads_view(mine[1]), heads_view(mine[2]), unit, unit, None)
    carry = absorb(carry, queries, heads_view(far[0]), heads_view(far[1]), key_scale, value_scale, keep)
    top, total, accum = carry
    result = (accum / total.T[:, :, None]).reshape(rows, local_heads * HEAD).astype(BF16)
    return lax.all_to_all(result, "uly", split_axis=0, concat_axis=1, tiled=True)


def general_shards(fresh_first, fresh_second, stale_cache, stale_exponent, text_first, text_second):
    local_heads = stale_exponent.shape[1] // lax.axis_size("uly")
    first_head = lax.axis_index("uly") * local_heads
    exponents = lax.dynamic_slice_in_dim(stale_exponent, first_head, local_heads, 1)
    scales = jnp.exp2(exponents.astype(F32))
    unit = jnp.ones((local_heads,), F32)
    mine_first = lax.all_to_all(fresh_first, "uly", split_axis=2, concat_axis=1, tiled=True)
    mine_second = lax.all_to_all(fresh_second, "uly", split_axis=2, concat_axis=1, tiled=True)
    rows = mine_first.shape[1]
    own_start = lax.axis_index("patch") * rows
    stale = lax.all_gather(stale_cache, "patch", axis=1, tiled=True)
    refreshed = lax.all_gather(mine_first[1:], "patch", axis=1, tiled=True)
    places = jnp.arange(stale.shape[1], dtype=jnp.int32)
    keep = (places < own_start) | (places >= own_start + rows)
    return (
        general_step(mine_first, text_first, stale, keep, scales[0], scales[1]),
        general_step(mine_second, text_second, refreshed, keep, unit, unit),
    )


def dot_t(a, b):
    return lax.dot_general(a, b, (((1,), (1,)), ((), ())), preferred_element_type=F32)


def dot(a, b):
    return jnp.dot(a, b, preferred_element_type=F32)


def scores_of(q, text, own, near, away, inside, key_factor):
    first, second = text[0].shape[0], near[0].shape[0]
    fixed = dot_t(q, jnp.concatenate([text[0], own[0]], 0)) * (LOG2E / HEAD**0.5)
    far = dot_t(q, jnp.concatenate([near[0], away[0]], 0)) * (key_factor * LOG2E)
    return jnp.concatenate([fixed[:, :first], jnp.where(inside, fixed[:, first:], far[:, :second]), far[:, second:]], 1)


def weights_of(score):
    weight = jnp.exp2(score - score.max(-1, keepdims=True))
    return weight.astype(BF16), weight.sum(-1, keepdims=True)


def mix(rounded, total, text, own, near, away, inside, value_factor):
    first, second = text[0].shape[0], near[0].shape[0]
    w_text, w_near, w_away = rounded[:, :first], rounded[:, first : first + second], rounded[:, first + second :]
    zero = jnp.zeros((), BF16)
    kept = dot(jnp.concatenate([w_text, jnp.where(inside, w_near, zero)], 1), jnp.concatenate([text[1], own[1]], 0))
    far = dot(jnp.concatenate([jnp.where(inside, zero, w_near), w_away], 1), jnp.concatenate([near[1], away[1]], 0))
    return (kept + value_factor * far) / total


def kernel_columns(ref, index):
    width = index[1]
    return ref.at[..., pl.ds(pl.multiple_of(index[0] * width, width), width)]


def run_copies(copies, sems):
    started = [pltpu.make_async_copy(a, b, sems.at[i]) for i, (a, b) in enumerate(copies)]
    for c in started:
        c.start()
    for c in started:
        c.wait()


def pack_shared_kernel(stale_ref, first_ref, *refs, layers):
    rounds = layers // 2
    layer = lax.axis_index("patch") // COLUMNS
    out_refs, sems = refs[:-1], refs[-1]
    width = out_refs[0].shape[-1]
    copies = [
        (kernel_columns(stale_ref, ((layer + k) % rounds, width)), out_refs[k]) for k in range(rounds)
    ]
    for s in range(layers):
        copies.append((kernel_columns(first_ref.at[1:], ((layer + s) % layers, width)), out_refs[rounds + s]))
    run_copies(copies, sems)


def pack_owned_kernel(first_ref, second_ref, text_first_ref, text_second_ref, *refs, layers):
    layer = lax.axis_index("patch") // COLUMNS
    out_refs, text_ref, sems = refs[:-2], refs[-2], refs[-1]
    width = text_ref.shape[-1]
    copies = []
    for s, out_ref in enumerate(out_refs):
        copies.append((kernel_columns(first_ref.at[:1], ((layer + s) % layers, width)), out_ref.at[:1]))
        copies.append((kernel_columns(second_ref, ((layer + s) % layers, width)), out_ref.at[1:]))
    for i, ref in enumerate((text_first_ref, text_second_ref)):
        copies.append((kernel_columns(ref, (layer % (layers // 2), width)), text_ref.at[2 * i : 2 * i + 2]))
    run_copies(copies, sems)


def pack(kernel, shapes, copies, *operands):
    return pl.pallas_call(
        kernel,
        out_shape=[jax.ShapeDtypeStruct(shape, BF16) for shape in shapes],
        in_specs=[pl.BlockSpec(memory_space=pl.ANY)] * len(operands),
        out_specs=[pl.BlockSpec(memory_space=pltpu.VMEM)] * len(shapes),
        scratch_shapes=[pltpu.SemaphoreType.DMA((copies,))],
        cost_estimate=pl.CostEstimate(flops=0, bytes_accessed=1 << 20, transcendentals=0),
    )(*operands)


def both_kernel(scale_ref, order_ref, queries_ref, text_ref, text_twin_ref, last_ref, last_twin_ref, *refs, parts, blocks, layers):
    sets, refs = [], list(refs)
    for p in parts:
        sets.append(refs[:p])
        refs = refs[p:]
    near_sets, away_sets = sets[:2], sets[2:]
    out_refs = refs
    rounds = layers // 2
    count, width = queries_ref.shape[1:]
    rows = count // layers
    first_row, last_row = blocks[0] * rows, (blocks[-1] + 1) * rows
    inverse = 1.0 / HEAD**0.5
    shape = (last_row - first_row, 2 * count)
    query_block = lax.broadcasted_iota(jnp.int32, shape, 0) // rows + blocks[0]
    place = lax.broadcasted_iota(jnp.int32, shape, 1)
    inside = [query_block == place // (2 * rows), query_block == place % count // rows]

    def fresh_view(pieces):
        return (pieces[1], 0) if len(pieces) == 2 else (pieces[0], layers)

    work = []
    for step in range(2):
        for head in range(width // HEAD):
            lanes = slice(head * HEAD, (head + 1) * HEAD)

            def text(i):
                at = 2 * step + i
                return jnp.where(order_ref[2, 0] == 0, text_ref[at, :, lanes], text_twin_ref[at, :, lanes])

            def fresh(pieces, i):
                ref, base = fresh_view(pieces)
                half = layers // 2
                return jnp.concatenate([ref[base + half * i + j, :, lanes] for j in range(half)], 0)

            def fresh_all(pair, i):
                return jnp.concatenate([fresh(p, i) for p in pair], 0)

            def in_patches(i):
                own, twin = (fresh(p, i) for p in near_sets)
                return jnp.concatenate([x[s * rows : (s + 1) * rows] for s in range(layers) for x in (own, twin)], 0)

            def last(i):
                return jnp.concatenate([last_ref[2 + i, :, lanes], last_twin_ref[last_twin_ref.shape[0] - 2 + i, :, lanes]], 0)

            def stale_in_patches(i):
                blocks = []
                for s in range(layers):
                    at = 2 * order_ref[1, s] + i
                    blocks.append(jnp.where(order_ref[0, s] == 0, *(p[0][at, :, lanes] for p in near_sets)))
                return jnp.concatenate(blocks, 0)

            def stale_elsewhere(i):
                return jnp.concatenate([p[0][2 * k + i, :, lanes] for p in away_sets for k in range(rounds)], 0)

            if step == 0:
                own = [in_patches(i) for i in range(2)]
                near = [stale_in_patches(i) for i in range(2)]
                away = [stale_elsewhere(i) for i in range(2)]
            else:
                own = [last(i) for i in range(2)]
                near = [fresh_all(near_sets, i) for i in range(2)]
                away = [fresh_all(away_sets, i) for i in range(2)]
            parts_of = ([text(i) for i in range(2)], own, near, away)
            work.append((step, head, lanes, parts_of))
    scores = [
        scores_of(queries_ref[step, first_row:last_row, lanes], *p, inside[step], inverse if step else scale_ref[0, head] * inverse)
        for step, head, lanes, p in work
    ]
    weights = [weights_of(s) for s in scores]
    for (step, head, lanes, p), (rounded, total) in zip(work, weights):
        result = mix(rounded, total, *p, inside[step], 1.0 if step else scale_ref[1, head])
        for i, out_ref in enumerate(out_refs):
            out_ref[step, :, lanes] = result[i * rows : (i + 1) * rows].astype(BF16)


def call_both(layers, scalars, parts, blocks, *operands):
    count, width = operands[0].shape[1:]
    rows = count // layers
    keys = 2 * operands[1].shape[1] + 8 * count
    in_vmem = pl.BlockSpec(memory_space=pltpu.VMEM)
    return pl.pallas_call(
        functools.partial(both_kernel, parts=parts, blocks=blocks, layers=layers),
        out_shape=[jax.ShapeDtypeStruct((2, rows, width), BF16)] * len(blocks),
        in_specs=[pl.BlockSpec(memory_space=pltpu.SMEM)] * len(scalars) + [in_vmem] * len(operands),
        out_specs=[in_vmem] * len(blocks),
        compiler_params=pltpu.CompilerParams(vmem_limit_bytes=12 * 1024 * 1024),
        cost_estimate=pl.CostEstimate(
            flops=4 * rows * len(blocks) * keys * width,
            bytes_accessed=4 * width * (keys + count),
            transcendentals=rows * len(blocks) * keys * width // HEAD,
        ),
    )(*scalars, *operands)


def layered_shards(layers, fresh_first, fresh_second, stale_cache, stale_exponent, text_first, text_second):
    core = lax.axis_index("uly")
    layer = lax.axis_index("patch") // COLUMNS
    rows, features = fresh_first.shape[1:]
    width = features // layers
    heads = width // HEAD
    half = features // 2
    rounds = layers // 2
    count = layers * rows
    text_rows = text_first.shape[1]

    def after(x, *needed):
        return lax.optimization_barrier((x,) + needed)[0]

    def layer_swap(x, shift):
        pairs = [(z * COLUMNS + y, (z + shift) % layers * COLUMNS + y) for z in range(layers) for y in range(COLUMNS)]
        return x if shift == 0 else lax.ppermute(x, "patch", pairs)

    def stale_round(x, k):
        pairs = []
        for z in range(layers):
            for y in range(COLUMNS):
                for u in range(2):
                    to = (u * rounds + (z + k) % rounds) * COLUMNS + y
                    pairs.append(((z * COLUMNS + y) * 2 + u, to * 2 + z // rounds))
        return lax.ppermute(x, ("patch", "uly"), pairs)

    def other_column(x):
        return lax.ppermute(x, "patch", [(p, p ^ 1) for p in range(layers * COLUMNS)])

    def other_core(x):
        return lax.ppermute(x, "uly", [(0, 1), (1, 0)])

    def columns_of(x, index):
        return lax.dynamic_slice_in_dim(x, index * width, width, x.ndim - 1)

    shared = [columns_of(stale_cache, (layer + k) % rounds) for k in range(rounds)]
    away_parts = [columns_of(fresh_first[1:], (layer + s) % layers) for s in range(1, layers)]
    shared += [columns_of(after(fresh_first, *away_parts)[1:], layer), *away_parts]
    *owned, text = pack(
        functools.partial(pack_owned_kernel, layers=layers),
        [(4, rows, width)] * layers + [(4, text_rows, width)],
        2 * layers + 2,
        after(fresh_first, shared),
        fresh_second,
        text_first,
        text_second,
    )
    stale = [stale_round(shared[k], k) for k in range(rounds)]
    fresh = [layer_swap(shared[rounds + s], s) for s in range(layers)]
    fresh[0] = after(fresh[0], owned)
    fresh_block = jnp.concatenate(fresh, 1).reshape(layers, 2 * rows, width)
    stale_block = jnp.concatenate(stale, 0)
    near = jnp.concatenate([stale_block, fresh_block], 0)
    away = [other_column(near)]
    owned = [owned[0], owned[1], after(owned[2], near), after(owned[3], near)]
    owned = {s: layer_swap(owned[s], s) for s in (0, 3, 2, 1)}
    owned = [owned[s] for s in range(layers)]
    away_twin = [other_core(away[0][:layers]), other_core(away[0][layers:])]
    last = jnp.concatenate(owned, 1)
    near_twin = [other_core(after(near, owned[1]))]
    last_twin = other_core(last)
    text_twin = other_core(after(text, owned[1]))
    sets = [[near], near_twin, away, away_twin]

    scales = jnp.exp2(lax.dynamic_slice_in_dim(stale_exponent, layer * heads, heads, 1).astype(F32))
    source = [(layer - s) % layers for s in range(layers)]
    order = jnp.stack(
        [jnp.stack([(L // rounds != core).astype(jnp.int32) for L in source]), jnp.stack([(L - layer) % rounds for L in source]), jnp.full((layers,), (layer // rounds != core).astype(jnp.int32))]
    )
    parts = tuple(len(p) for p in sets)
    flat = [p for pieces in sets for p in pieces]
    operands = [last[:2], text, text_twin, last, last_twin, *flat]
    sent = call_both(layers, [scales, order], parts, tuple(range(1, layers)), *operands)
    (kept,) = call_both(layers, [scales, order], parts, (0,), *operands)
    blocks = [kept, *sent]

    out = jnp.zeros((2, rows, features), BF16)
    for s in (0, 2, 3, 1):
        out = lax.dynamic_update_slice_in_dim(out, layer_swap(blocks[s], -s), (layer + s) % layers * width, 2)
    return out[0], out[1]


def solution(mesh):
    placed = (
        P(None, ("group", "patch", "uly"), None),
        P(None, ("group", "patch", "uly"), None),
        P(None, ("group", "patch"), "uly"),
        P("group", None),
        P(None, "group", "uly"),
        P(None, "group", "uly"),
    )

    def shards(*arrays):
        layers = mesh.shape["patch"] // COLUMNS
        heads = arrays[0].shape[2] // HEAD
        if mesh.shape["uly"] == 2 and layers == 4 and heads % layers == 0:
            return layered_shards(layers, *arrays)
        return general_shards(*arrays)

    return jax.shard_map(
        shards,
        mesh=mesh,
        in_specs=placed,
        out_specs=(P(("group", "patch", "uly"), None), P(("group", "patch", "uly"), None)),
        check_vma=False,
    )
```

```python
import functools

import jax
import jax.numpy as jnp
from jax import lax
from jax.experimental import pallas as pl
from jax.experimental.pallas import tpu as pltpu
from jax.sharding import PartitionSpec as P

HEAD = 128
LOG2E = 1.4426950408889634
COLUMNS = 2
BF16 = jnp.bfloat16
F32 = jnp.float32


def heads_view(array):
    return array.reshape(array.shape[0], array.shape[1] // HEAD, HEAD)


def absorb(carry, queries, keys_rows, values, key_scale, value_scale, keep):
    top, total, accum = carry
    inverse = 1.0 / HEAD**0.5
    score = jnp.einsum("qhd,khd->hqk", queries, keys_rows, preferred_element_type=F32)
    score = score * (key_scale * inverse)[:, None, None]
    if keep is not None:
        score = jnp.where(keep[None, None, :], score, -jnp.inf)
    new_top = jnp.maximum(top, score.max(-1))
    fade = jnp.exp(top - new_top)
    weight = jnp.exp(score - new_top[:, :, None])
    total = total * fade + weight.sum(-1)
    addend = jnp.einsum("hqk,khd->qhd", weight.astype(BF16), values, preferred_element_type=F32)
    accum = accum * fade.T[:, :, None] + addend * value_scale[None, :, None]
    return (new_top, total, accum)


def general_step(mine, text, far, keep, key_scale, value_scale):
    queries = heads_view(mine[0])
    rows, local_heads = queries.shape[:2]
    unit = jnp.ones((local_heads,), F32)
    carry = (
        jnp.full((local_heads, rows), -jnp.inf, F32),
        jnp.zeros((local_heads, rows), F32),
        jnp.zeros((rows, local_heads, HEAD), F32),
    )
    carry = absorb(carry, queries, heads_view(text[0]), heads_view(text[1]), unit, unit, None)
    carry = absorb(carry, queries, heads_view(mine[1]), heads_view(mine[2]), unit, unit, None)
    carry = absorb(carry, queries, heads_view(far[0]), heads_view(far[1]), key_scale, value_scale, keep)
    top, total, accum = carry
    result = (accum / total.T[:, :, None]).reshape(rows, local_heads * HEAD).astype(BF16)
    return lax.all_to_all(result, "uly", split_axis=0, concat_axis=1, tiled=True)


def general_shards(fresh_first, fresh_second, stale_cache, stale_exponent, text_first, text_second):
    local_heads = stale_exponent.shape[1] // lax.axis_size("uly")
    first_head = lax.axis_index("uly") * local_heads
    exponents = lax.dynamic_slice_in_dim(stale_exponent, first_head, local_heads, 1)
    scales = jnp.exp2(exponents.astype(F32))
    unit = jnp.ones((local_heads,), F32)
    mine_first = lax.all_to_all(fresh_first, "uly", split_axis=2, concat_axis=1, tiled=True)
    mine_second = lax.all_to_all(fresh_second, "uly", split_axis=2, concat_axis=1, tiled=True)
    rows = mine_first.shape[1]
    own_start = lax.axis_index("patch") * rows
    stale = lax.all_gather(stale_cache, "patch", axis=1, tiled=True)
    refreshed = lax.all_gather(mine_first[1:], "patch", axis=1, tiled=True)
    places = jnp.arange(stale.shape[1], dtype=jnp.int32)
    keep = (places < own_start) | (places >= own_start + rows)
    return (
        general_step(mine_first, text_first, stale, keep, scales[0], scales[1]),
        general_step(mine_second, text_second, refreshed, keep, unit, unit),
    )


def dot_t(a, b):
    return lax.dot_general(a, b, (((1,), (1,)), ((), ())), preferred_element_type=F32)


def dot(a, b):
    return jnp.dot(a, b, preferred_element_type=F32)


def scores_of(q, text, own, near, away, inside, key_factor):
    first, second = text[0].shape[0], near[0].shape[0]
    fixed = dot_t(q, jnp.concatenate([text[0], own[0]], 0)) * (LOG2E / HEAD**0.5)
    far = dot_t(q, jnp.concatenate([near[0], away[0]], 0)) * (key_factor * LOG2E)
    return jnp.concatenate([fixed[:, :first], jnp.where(inside, fixed[:, first:], far[:, :second]), far[:, second:]], 1)


def weights_of(score):
    weight = jnp.exp2(score - score.max(-1, keepdims=True))
    return weight.astype(BF16), weight.sum(-1, keepdims=True)


def mix(rounded, total, text, own, near, away, inside, value_factor):
    first, second = text[0].shape[0], near[0].shape[0]
    w_text, w_near, w_away = rounded[:, :first], rounded[:, first : first + second], rounded[:, first + second :]
    zero = jnp.zeros((), BF16)
    kept = dot(jnp.concatenate([w_text, jnp.where(inside, w_near, zero)], 1), jnp.concatenate([text[1], own[1]], 0))
    far = dot(jnp.concatenate([jnp.where(inside, zero, w_near), w_away], 1), jnp.concatenate([near[1], away[1]], 0))
    return (kept + value_factor * far) / total


def kernel_columns(ref, index):
    width = index[1]
    return ref.at[..., pl.ds(pl.multiple_of(index[0] * width, width), width)]


def run_copies(copies, sems):
    started = [pltpu.make_async_copy(a, b, sems.at[i]) for i, (a, b) in enumerate(copies)]
    for c in started:
        c.start()
    for c in started:
        c.wait()


def pack_shared_kernel(stale_ref, first_ref, *refs, layers):
    rounds = layers // 2
    layer = lax.axis_index("patch") // COLUMNS
    out_refs, sems = refs[:-1], refs[-1]
    width = out_refs[0].shape[-1]
    copies = [
        (kernel_columns(stale_ref, ((layer + k) % rounds, width)), out_refs[k]) for k in range(rounds)
    ]
    for s in range(layers):
        copies.append((kernel_columns(first_ref.at[1:], ((layer + s) % layers, width)), out_refs[rounds + s]))
    run_copies(copies, sems)


def pack_owned_kernel(first_ref, second_ref, text_first_ref, text_second_ref, *refs, layers):
    layer = lax.axis_index("patch") // COLUMNS
    out_refs, text_ref, sems = refs[:-2], refs[-2], refs[-1]
    width = text_ref.shape[-1]
    copies = []
    for s, out_ref in enumerate(out_refs):
        copies.append((kernel_columns(first_ref.at[:1], ((layer + s) % layers, width)), out_ref.at[:1]))
        copies.append((kernel_columns(second_ref, ((layer + s) % layers, width)), out_ref.at[1:]))
    for i, ref in enumerate((text_first_ref, text_second_ref)):
        copies.append((kernel_columns(ref, (layer % (layers // 2), width)), text_ref.at[2 * i : 2 * i + 2]))
    run_copies(copies, sems)


def pack(kernel, shapes, copies, *operands):
    return pl.pallas_call(
        kernel,
        out_shape=[jax.ShapeDtypeStruct(shape, BF16) for shape in shapes],
        in_specs=[pl.BlockSpec(memory_space=pl.ANY)] * len(operands),
        out_specs=[pl.BlockSpec(memory_space=pltpu.VMEM)] * len(shapes),
        scratch_shapes=[pltpu.SemaphoreType.DMA((copies,))],
        cost_estimate=pl.CostEstimate(flops=0, bytes_accessed=1 << 20, transcendentals=0),
    )(*operands)


def both_kernel(scale_ref, order_ref, queries_ref, text_ref, text_twin_ref, last_ref, last_twin_ref, *refs, parts, blocks, layers):
    sets, refs = [], list(refs)
    for p in parts:
        sets.append(refs[:p])
        refs = refs[p:]
    near_sets, away_sets = sets[:2], sets[2:]
    out_refs = refs
    rounds = layers // 2
    count, width = queries_ref.shape[1:]
    rows = count // layers
    first_row, last_row = blocks[0] * rows, (blocks[-1] + 1) * rows
    inverse = 1.0 / HEAD**0.5
    shape = (last_row - first_row, 2 * count)
    query_block = lax.broadcasted_iota(jnp.int32, shape, 0) // rows + blocks[0]
    place = lax.broadcasted_iota(jnp.int32, shape, 1)
    inside = [query_block == place // (2 * rows), query_block == place % count // rows]

    def fresh_view(pieces):
        return (pieces[1], 0) if len(pieces) == 2 else (pieces[0], layers)

    work = []
    for step in range(2):
        for head in range(width // HEAD):
            lanes = slice(head * HEAD, (head + 1) * HEAD)

            def text(i):
                at = 2 * step + i
                return jnp.where(order_ref[2, 0] == 0, text_ref[at, :, lanes], text_twin_ref[at, :, lanes])

            def fresh(pieces, i):
                ref, base = fresh_view(pieces)
                half = layers // 2
                return jnp.concatenate([ref[base + half * i + j, :, lanes] for j in range(half)], 0)

            def fresh_all(pair, i):
                return jnp.concatenate([fresh(p, i) for p in pair], 0)

            def in_patches(i):
                own, twin = (fresh(p, i) for p in near_sets)
                return jnp.concatenate([x[s * rows : (s + 1) * rows] for s in range(layers) for x in (own, twin)], 0)

            def last(i):
                return jnp.concatenate([last_ref[2 + i, :, lanes], last_twin_ref[last_twin_ref.shape[0] - 2 + i, :, lanes]], 0)

            def stale_in_patches(i):
                blocks = []
                for s in range(layers):
                    at = 2 * order_ref[1, s] + i
                    blocks.append(jnp.where(order_ref[0, s] == 0, *(p[0][at, :, lanes] for p in near_sets)))
                return jnp.concatenate(blocks, 0)

            def stale_elsewhere(i):
                return jnp.concatenate([p[0][2 * k + i, :, lanes] for p in away_sets for k in range(rounds)], 0)

            if step == 0:
                own = [in_patches(i) for i in range(2)]
                near = [stale_in_patches(i) for i in range(2)]
                away = [stale_elsewhere(i) for i in range(2)]
            else:
                own = [last(i) for i in range(2)]
                near = [fresh_all(near_sets, i) for i in range(2)]
                away = [fresh_all(away_sets, i) for i in range(2)]
            parts_of = ([text(i) for i in range(2)], own, near, away)
            work.append((step, head, lanes, parts_of))
    scores = [
        scores_of(queries_ref[step, first_row:last_row, lanes], *p, inside[step], inverse if step else scale_ref[0, head] * inverse)
        for step, head, lanes, p in work
    ]
    weights = [weights_of(s) for s in scores]
    for (step, head, lanes, p), (rounded, total) in zip(work, weights):
        result = mix(rounded, total, *p, inside[step], 1.0 if step else scale_ref[1, head])
        for i, out_ref in enumerate(out_refs):
            out_ref[step, :, lanes] = result[i * rows : (i + 1) * rows].astype(BF16)


def call_both(layers, scalars, parts, blocks, *operands):
    count, width = operands[0].shape[1:]
    rows = count // layers
    keys = 2 * operands[1].shape[1] + 8 * count
    in_vmem = pl.BlockSpec(memory_space=pltpu.VMEM)
    return pl.pallas_call(
        functools.partial(both_kernel, parts=parts, blocks=blocks, layers=layers),
        out_shape=[jax.ShapeDtypeStruct((2, rows, width), BF16)] * len(blocks),
        in_specs=[pl.BlockSpec(memory_space=pltpu.SMEM)] * len(scalars) + [in_vmem] * len(operands),
        out_specs=[in_vmem] * len(blocks),
        compiler_params=pltpu.CompilerParams(vmem_limit_bytes=12 * 1024 * 1024),
        cost_estimate=pl.CostEstimate(
            flops=4 * rows * len(blocks) * keys * width,
            bytes_accessed=4 * width * (keys + count),
            transcendentals=rows * len(blocks) * keys * width // HEAD,
        ),
    )(*scalars, *operands)


def layered_shards(layers, fresh_first, fresh_second, stale_cache, stale_exponent, text_first, text_second):
    core = lax.axis_index("uly")
    layer = lax.axis_index("patch") // COLUMNS
    rows, features = fresh_first.shape[1:]
    width = features // layers
    heads = width // HEAD
    half = features // 2
    rounds = layers // 2
    count = layers * rows
    text_rows = text_first.shape[1]

    def after(x, *needed):
        return lax.optimization_barrier((x,) + needed)[0]

    def layer_swap(x, shift):
        pairs = [(z * COLUMNS + y, (z + shift) % layers * COLUMNS + y) for z in range(layers) for y in range(COLUMNS)]
        return x if shift == 0 else lax.ppermute(x, "patch", pairs)

    def stale_round(x, k):
        pairs = []
        for z in range(layers):
            for y in range(COLUMNS):
                for u in range(2):
                    to = (u * rounds + (z + k) % rounds) * COLUMNS + y
                    pairs.append(((z * COLUMNS + y) * 2 + u, to * 2 + z // rounds))
        return lax.ppermute(x, ("patch", "uly"), pairs)

    def other_column(x):
        return lax.ppermute(x, "patch", [(p, p ^ 1) for p in range(layers * COLUMNS)])

    def other_core(x):
        return lax.ppermute(x, "uly", [(0, 1), (1, 0)])

    def columns_of(x, index):
        return lax.dynamic_slice_in_dim(x, index * width, width, x.ndim - 1)

    shared = [columns_of(stale_cache, (layer + k) % rounds) for k in range(rounds)]
    away_parts = [columns_of(fresh_first[1:], (layer + s) % layers) for s in range(1, layers)]
    shared += [columns_of(after(fresh_first, *away_parts)[1:], layer), *away_parts]
    *owned, text = pack(
        functools.partial(pack_owned_kernel, layers=layers),
        [(4, rows, width)] * layers + [(4, text_rows, width)],
        2 * layers + 2,
        after(fresh_first, shared),
        fresh_second,
        text_first,
        text_second,
    )
    stale = [stale_round(shared[k], k) for k in range(rounds)]
    fresh = [layer_swap(shared[rounds + s], s) for s in range(layers)]
    fresh[0] = after(fresh[0], owned)
    fresh_block = jnp.concatenate(fresh, 1).reshape(layers, 2 * rows, width)
    stale_block = jnp.concatenate(stale, 0)
    near = jnp.concatenate([stale_block, fresh_block], 0)
    away = [other_column(near)]
    owned = [owned[0], owned[1], after(owned[2], near), after(owned[3], near)]
    owned = {s: layer_swap(owned[s], s) for s in (0, 3, 2, 1)}
    owned = [owned[s] for s in range(layers)]
    away_twin = [other_core(away[0][:layers]), other_core(away[0][layers:])]
    last = jnp.concatenate(owned, 1)
    near_twin = [other_core(after(near, owned[1]))]
    last_twin = other_core(last)
    text_twin = other_core(text)
    sets = [[near], near_twin, away, away_twin]

    scales = jnp.exp2(lax.dynamic_slice_in_dim(stale_exponent, layer * heads, heads, 1).astype(F32))
    source = [(layer - s) % layers for s in range(layers)]
    order = jnp.stack(
        [jnp.stack([(L // rounds != core).astype(jnp.int32) for L in source]), jnp.stack([(L - layer) % rounds for L in source]), jnp.full((layers,), (layer // rounds != core).astype(jnp.int32))]
    )
    parts = tuple(len(p) for p in sets)
    flat = [p for pieces in sets for p in pieces]
    operands = [last[:2], text, text_twin, last, last_twin, *flat]
    sent = call_both(layers, [scales, order], parts, tuple(range(1, layers)), *operands)
    (kept,) = call_both(layers, [scales, order], parts, (0,), *operands)
    blocks = [kept, *sent]

    out = jnp.zeros((2, rows, features), BF16)
    for s in (0, 2, 3, 1):
        out = lax.dynamic_update_slice_in_dim(out, layer_swap(blocks[s], -s), (layer + s) % layers * width, 2)
    return out[0], out[1]


def solution(mesh):
    placed = (
        P(None, ("group", "patch", "uly"), None),
        P(None, ("group", "patch", "uly"), None),
        P(None, ("group", "patch"), "uly"),
        P("group", None),
        P(None, "group", "uly"),
        P(None, "group", "uly"),
    )

    def shards(*arrays):
        layers = mesh.shape["patch"] // COLUMNS
        heads = arrays[0].shape[2] // HEAD
        if mesh.shape["uly"] == 2 and layers == 4 and heads % layers == 0:
            return layered_shards(layers, *arrays)
        return general_shards(*arrays)

    return jax.shard_map(
        shards,
        mesh=mesh,
        in_specs=placed,
        out_specs=(P(("group", "patch", "uly"), None), P(("group", "patch", "uly"), None)),
        check_vma=False,
    )
```

```python
import functools

import jax
import jax.numpy as jnp
from jax import lax
from jax.experimental import pallas as pl
from jax.experimental.pallas import tpu as pltpu
from jax.sharding import PartitionSpec as P

HEAD = 128
LOG2E = 1.4426950408889634
COLUMNS = 2
BF16 = jnp.bfloat16
F32 = jnp.float32


def heads_view(array):
    return array.reshape(array.shape[0], array.shape[1] // HEAD, HEAD)


def absorb(carry, queries, keys_rows, values, key_scale, value_scale, keep):
    top, total, accum = carry
    inverse = 1.0 / HEAD**0.5
    score = jnp.einsum("qhd,khd->hqk", queries, keys_rows, preferred_element_type=F32)
    score = score * (key_scale * inverse)[:, None, None]
    if keep is not None:
        score = jnp.where(keep[None, None, :], score, -jnp.inf)
    new_top = jnp.maximum(top, score.max(-1))
    fade = jnp.exp(top - new_top)
    weight = jnp.exp(score - new_top[:, :, None])
    total = total * fade + weight.sum(-1)
    addend = jnp.einsum("hqk,khd->qhd", weight.astype(BF16), values, preferred_element_type=F32)
    accum = accum * fade.T[:, :, None] + addend * value_scale[None, :, None]
    return (new_top, total, accum)


def general_step(mine, text, far, keep, key_scale, value_scale):
    queries = heads_view(mine[0])
    rows, local_heads = queries.shape[:2]
    unit = jnp.ones((local_heads,), F32)
    carry = (
        jnp.full((local_heads, rows), -jnp.inf, F32),
        jnp.zeros((local_heads, rows), F32),
        jnp.zeros((rows, local_heads, HEAD), F32),
    )
    carry = absorb(carry, queries, heads_view(text[0]), heads_view(text[1]), unit, unit, None)
    carry = absorb(carry, queries, heads_view(mine[1]), heads_view(mine[2]), unit, unit, None)
    carry = absorb(carry, queries, heads_view(far[0]), heads_view(far[1]), key_scale, value_scale, keep)
    top, total, accum = carry
    result = (accum / total.T[:, :, None]).reshape(rows, local_heads * HEAD).astype(BF16)
    return lax.all_to_all(result, "uly", split_axis=0, concat_axis=1, tiled=True)


def general_shards(fresh_first, fresh_second, stale_cache, stale_exponent, text_first, text_second):
    local_heads = stale_exponent.shape[1] // lax.axis_size("uly")
    first_head = lax.axis_index("uly") * local_heads
    exponents = lax.dynamic_slice_in_dim(stale_exponent, first_head, local_heads, 1)
    scales = jnp.exp2(exponents.astype(F32))
    unit = jnp.ones((local_heads,), F32)
    mine_first = lax.all_to_all(fresh_first, "uly", split_axis=2, concat_axis=1, tiled=True)
    mine_second = lax.all_to_all(fresh_second, "uly", split_axis=2, concat_axis=1, tiled=True)
    rows = mine_first.shape[1]
    own_start = lax.axis_index("patch") * rows
    stale = lax.all_gather(stale_cache, "patch", axis=1, tiled=True)
    refreshed = lax.all_gather(mine_first[1:], "patch", axis=1, tiled=True)
    places = jnp.arange(stale.shape[1], dtype=jnp.int32)
    keep = (places < own_start) | (places >= own_start + rows)
    return (
        general_step(mine_first, text_first, stale, keep, scales[0], scales[1]),
        general_step(mine_second, text_second, refreshed, keep, unit, unit),
    )


def dot_t(a, b):
    return lax.dot_general(a, b, (((1,), (1,)), ((), ())), preferred_element_type=F32)


def dot(a, b):
    return jnp.dot(a, b, preferred_element_type=F32)


def scores_of(q, text, own, near, away, inside, key_factor):
    first, second = text[0].shape[0], near[0].shape[0]
    fixed = dot_t(q, jnp.concatenate([text[0], own[0]], 0)) * (LOG2E / HEAD**0.5)
    far = dot_t(q, jnp.concatenate([near[0], away[0]], 0)) * (key_factor * LOG2E)
    return jnp.concatenate([fixed[:, :first], jnp.where(inside, fixed[:, first:], far[:, :second]), far[:, second:]], 1)


def weights_of(score):
    weight = jnp.exp2(score - score.max(-1, keepdims=True))
    return weight.astype(BF16), weight.sum(-1, keepdims=True)


def mix(rounded, total, text, own, near, away, inside, value_factor):
    first, second = text[0].shape[0], near[0].shape[0]
    w_text, w_near, w_away = rounded[:, :first], rounded[:, first : first + second], rounded[:, first + second :]
    zero = jnp.zeros((), BF16)
    kept = dot(jnp.concatenate([w_text, jnp.where(inside, w_near, zero)], 1), jnp.concatenate([text[1], own[1]], 0))
    far = dot(jnp.concatenate([jnp.where(inside, zero, w_near), w_away], 1), jnp.concatenate([near[1], away[1]], 0))
    return (kept + value_factor * far) / total


def kernel_columns(ref, index):
    width = index[1]
    return ref.at[..., pl.ds(pl.multiple_of(index[0] * width, width), width)]


def run_copies(copies, sems):
    started = [pltpu.make_async_copy(a, b, sems.at[i]) for i, (a, b) in enumerate(copies)]
    for c in started:
        c.start()
    for c in started:
        c.wait()


def pack_shared_kernel(stale_ref, first_ref, *refs, layers):
    rounds = layers // 2
    layer = lax.axis_index("patch") // COLUMNS
    out_refs, sems = refs[:-1], refs[-1]
    width = out_refs[0].shape[-1]
    copies = [
        (kernel_columns(stale_ref, ((layer + k) % rounds, width)), out_refs[k]) for k in range(rounds)
    ]
    for s in range(layers):
        copies.append((kernel_columns(first_ref.at[1:], ((layer + s) % layers, width)), out_refs[rounds + s]))
    run_copies(copies, sems)


def pack_owned_kernel(first_ref, second_ref, text_first_ref, text_second_ref, *refs, layers):
    layer = lax.axis_index("patch") // COLUMNS
    out_refs, text_ref, sems = refs[:-2], refs[-2], refs[-1]
    width = text_ref.shape[-1]
    copies = []
    for s, out_ref in enumerate(out_refs):
        copies.append((kernel_columns(first_ref.at[:1], ((layer + s) % layers, width)), out_ref.at[:1]))
        copies.append((kernel_columns(second_ref, ((layer + s) % layers, width)), out_ref.at[1:]))
    for i, ref in enumerate((text_first_ref, text_second_ref)):
        copies.append((kernel_columns(ref, (layer % (layers // 2), width)), text_ref.at[2 * i : 2 * i + 2]))
    run_copies(copies, sems)


def pack(kernel, shapes, copies, *operands):
    return pl.pallas_call(
        kernel,
        out_shape=[jax.ShapeDtypeStruct(shape, BF16) for shape in shapes],
        in_specs=[pl.BlockSpec(memory_space=pl.ANY)] * len(operands),
        out_specs=[pl.BlockSpec(memory_space=pltpu.VMEM)] * len(shapes),
        scratch_shapes=[pltpu.SemaphoreType.DMA((copies,))],
        cost_estimate=pl.CostEstimate(flops=0, bytes_accessed=1 << 20, transcendentals=0),
    )(*operands)


def both_kernel(scale_ref, order_ref, queries_ref, text_ref, text_twin_ref, last_ref, last_twin_ref, *refs, parts, blocks, layers):
    sets, refs = [], list(refs)
    for p in parts:
        sets.append(refs[:p])
        refs = refs[p:]
    near_sets, away_sets = sets[:2], sets[2:]
    out_refs = refs
    rounds = layers // 2
    count, width = queries_ref.shape[1:]
    rows = count // layers
    first_row, last_row = blocks[0] * rows, (blocks[-1] + 1) * rows
    inverse = 1.0 / HEAD**0.5
    shape = (last_row - first_row, 2 * count)
    query_block = lax.broadcasted_iota(jnp.int32, shape, 0) // rows + blocks[0]
    place = lax.broadcasted_iota(jnp.int32, shape, 1)
    inside = [query_block == place // (2 * rows), query_block == place % count // rows]

    def fresh_view(pieces):
        return (pieces[1], 0) if len(pieces) == 2 else (pieces[0], layers)

    work = []
    for step in range(2):
        for head in range(width // HEAD):
            lanes = slice(head * HEAD, (head + 1) * HEAD)

            def text(i):
                at = 2 * step + i
                return jnp.where(order_ref[2, 0] == 0, text_ref[at, :, lanes], text_twin_ref[at, :, lanes])

            def fresh(pieces, i):
                ref, base = fresh_view(pieces)
                half = layers // 2
                return jnp.concatenate([ref[base + half * i + j, :, lanes] for j in range(half)], 0)

            def fresh_all(pair, i):
                return jnp.concatenate([fresh(p, i) for p in pair], 0)

            def in_patches(i):
                own, twin = (fresh(p, i) for p in near_sets)
                return jnp.concatenate([x[s * rows : (s + 1) * rows] for s in range(layers) for x in (own, twin)], 0)

            def last(i):
                return jnp.concatenate([last_ref[2 + i, :, lanes], last_twin_ref[last_twin_ref.shape[0] - 2 + i, :, lanes]], 0)

            def stale_in_patches(i):
                blocks = []
                for s in range(layers):
                    at = 2 * order_ref[1, s] + i
                    blocks.append(jnp.where(order_ref[0, s] == 0, *(p[0][at, :, lanes] for p in near_sets)))
                return jnp.concatenate(blocks, 0)

            def stale_elsewhere(i):
                return jnp.concatenate([p[0][2 * k + i, :, lanes] for p in away_sets for k in range(rounds)], 0)

            if step == 0:
                own = [in_patches(i) for i in range(2)]
                near = [stale_in_patches(i) for i in range(2)]
                away = [stale_elsewhere(i) for i in range(2)]
            else:
                own = [last(i) for i in range(2)]
                near = [fresh_all(near_sets, i) for i in range(2)]
                away = [fresh_all(away_sets, i) for i in range(2)]
            parts_of = ([text(i) for i in range(2)], own, near, away)
            work.append((step, head, lanes, parts_of))
    scores = [
        scores_of(queries_ref[step, first_row:last_row, lanes], *p, inside[step], inverse if step else scale_ref[0, head] * inverse)
        for step, head, lanes, p in work
    ]
    weights = [weights_of(s) for s in scores]
    for (step, head, lanes, p), (rounded, total) in zip(work, weights):
        result = mix(rounded, total, *p, inside[step], 1.0 if step else scale_ref[1, head])
        for i, out_ref in enumerate(out_refs):
            out_ref[step, :, lanes] = result[i * rows : (i + 1) * rows].astype(BF16)


def call_both(layers, scalars, parts, blocks, *operands):
    count, width = operands[0].shape[1:]
    rows = count // layers
    keys = 2 * operands[1].shape[1] + 8 * count
    in_vmem = pl.BlockSpec(memory_space=pltpu.VMEM)
    return pl.pallas_call(
        functools.partial(both_kernel, parts=parts, blocks=blocks, layers=layers),
        out_shape=[jax.ShapeDtypeStruct((2, rows, width), BF16)] * len(blocks),
        in_specs=[pl.BlockSpec(memory_space=pltpu.SMEM)] * len(scalars) + [in_vmem] * len(operands),
        out_specs=[in_vmem] * len(blocks),
        compiler_params=pltpu.CompilerParams(vmem_limit_bytes=12 * 1024 * 1024),
        cost_estimate=pl.CostEstimate(
            flops=4 * rows * len(blocks) * keys * width,
            bytes_accessed=4 * width * (keys + count),
            transcendentals=rows * len(blocks) * keys * width // HEAD,
        ),
    )(*scalars, *operands)


def layered_shards(layers, fresh_first, fresh_second, stale_cache, stale_exponent, text_first, text_second):
    core = lax.axis_index("uly")
    layer = lax.axis_index("patch") // COLUMNS
    rows, features = fresh_first.shape[1:]
    width = features // layers
    heads = width // HEAD
    half = features // 2
    rounds = layers // 2
    count = layers * rows
    text_rows = text_first.shape[1]

    def after(x, *needed):
        return lax.optimization_barrier((x,) + needed)[0]

    def layer_swap(x, shift):
        pairs = [(z * COLUMNS + y, (z + shift) % layers * COLUMNS + y) for z in range(layers) for y in range(COLUMNS)]
        return x if shift == 0 else lax.ppermute(x, "patch", pairs)

    def stale_round(x, k):
        pairs = []
        for z in range(layers):
            for y in range(COLUMNS):
                for u in range(2):
                    to = (u * rounds + (z + k) % rounds) * COLUMNS + y
                    pairs.append(((z * COLUMNS + y) * 2 + u, to * 2 + z // rounds))
        return lax.ppermute(x, ("patch", "uly"), pairs)

    def other_column(x):
        return lax.ppermute(x, "patch", [(p, p ^ 1) for p in range(layers * COLUMNS)])

    def other_core(x):
        return lax.ppermute(x, "uly", [(0, 1), (1, 0)])

    def columns_of(x, index):
        return lax.dynamic_slice_in_dim(x, index * width, width, x.ndim - 1)

    shared = [columns_of(stale_cache, (layer + k) % rounds) for k in range(rounds)]
    away_parts = [columns_of(fresh_first[1:], (layer + s) % layers) for s in range(1, layers)]
    shared += [columns_of(after(fresh_first, *away_parts, *shared)[1:], layer), *away_parts]
    *owned, text = pack(
        functools.partial(pack_owned_kernel, layers=layers),
        [(4, rows, width)] * layers + [(4, text_rows, width)],
        2 * layers + 2,
        after(fresh_first, shared),
        fresh_second,
        text_first,
        text_second,
    )
    stale = [stale_round(shared[k], k) for k in range(rounds)]
    fresh = [layer_swap(shared[rounds + s], s) for s in range(layers)]
    fresh[0] = after(fresh[0], owned)
    fresh_block = jnp.concatenate(fresh, 1).reshape(layers, 2 * rows, width)
    stale_block = jnp.concatenate(stale, 0)
    near = jnp.concatenate([stale_block, fresh_block], 0)
    away = [other_column(near)]
    owned = [owned[0], owned[1], after(owned[2], near), after(owned[3], near)]
    owned = {s: layer_swap(owned[s], s) for s in (0, 3, 2, 1)}
    owned = [owned[s] for s in range(layers)]
    away_twin = [other_core(away[0][:layers]), other_core(away[0][layers:])]
    last = jnp.concatenate(owned, 1)
    near_twin = [other_core(after(near, owned[1]))]
    last_twin = other_core(last)
    text_twin = other_core(text)
    sets = [[near], near_twin, away, away_twin]

    scales = jnp.exp2(lax.dynamic_slice_in_dim(stale_exponent, layer * heads, heads, 1).astype(F32))
    source = [(layer - s) % layers for s in range(layers)]
    order = jnp.stack(
        [jnp.stack([(L // rounds != core).astype(jnp.int32) for L in source]), jnp.stack([(L - layer) % rounds for L in source]), jnp.full((layers,), (layer // rounds != core).astype(jnp.int32))]
    )
    parts = tuple(len(p) for p in sets)
    flat = [p for pieces in sets for p in pieces]
    operands = [last[:2], text, text_twin, last, last_twin, *flat]
    sent = call_both(layers, [scales, order], parts, tuple(range(1, layers)), *operands)
    (kept,) = call_both(layers, [scales, order], parts, (0,), *operands)
    blocks = [kept, *sent]

    out = jnp.zeros((2, rows, features), BF16)
    for s in (0, 2, 3, 1):
        out = lax.dynamic_update_slice_in_dim(out, layer_swap(blocks[s], -s), (layer + s) % layers * width, 2)
    return out[0], out[1]


def solution(mesh):
    placed = (
        P(None, ("group", "patch", "uly"), None),
        P(None, ("group", "patch", "uly"), None),
        P(None, ("group", "patch"), "uly"),
        P("group", None),
        P(None, "group", "uly"),
        P(None, "group", "uly"),
    )

    def shards(*arrays):
        layers = mesh.shape["patch"] // COLUMNS
        heads = arrays[0].shape[2] // HEAD
        if mesh.shape["uly"] == 2 and layers == 4 and heads % layers == 0:
            return layered_shards(layers, *arrays)
        return general_shards(*arrays)

    return jax.shard_map(
        shards,
        mesh=mesh,
        in_specs=placed,
        out_specs=(P(("group", "patch", "uly"), None), P(("group", "patch", "uly"), None)),
        check_vma=False,
    )
```
